32 devices in a mesh: groups: 2 (over x), dap: 16 (over z, y, core).
Axes of the slice: x: 2, y: 2, z: 4, core: 2. Of those that a mesh axis runs over, the one named last changes fastest.
Arguments:
- pair_state: bfloat16 [160, 80, 128], P(('groups', 'dap')), parts along dimension 0, may hold values from -6 to 6
- chain_index: int32 [160], P('groups'), parts along dimension 0, may hold values from 0 to 3, as said below
- pair_mask: int32 [160, 80], P(('groups', 'dap')), parts along dimension 0, may hold values 0 or 1
- chain_table: float32 [2, 128], replicated, may hold values from -4 to 4
- norm_gain: float32 [2, 2, 128], replicated, may hold values from 0.1 to 1.9
- norm_shift: float32 [2, 2, 128], replicated, may hold values from -3 to 3
- projections: bfloat16 [2, 5, 128, 128], replicated, may hold values from -0.5 to 0.5
- output_weight: bfloat16 [2, 128, 128], replicated, may hold values from -0.5 to 0.5
- cotangent: bfloat16 [160, 80, 128], P(('groups', 'dap')), parts along dimension 0, may hold values from -6 to 6
Outputs:
- grad_pair: bfloat16 [160, 80, 128], P(('groups', 'dap')), parts along dimension 0
- projection_grads: float32 [4, 5, 128, 128], P('groups'), parts along dimension 0
- output_weight_grad: float32 [4, 128, 128], P('groups'), parts along dimension 0
The draws below stay inside these ranges and needn't reach their ends.
There are 2 independent parts, one for each index of `groups`. The reference program is written for one: setup_inputs(seed, part) draws one part's arguments, and reference() takes and returns one part's arrays. A program takes and returns all parts, laid end to end along the dimension named above; an argument that names none is the same for every part. Nothing has to cross between parts.
Inputs may be any that keep to these rules, and one draw needn't show every extreme that they name: `chain_index`: the chain index never decreases along the residues, and every chain has at least one residue.
All inputs are finite; a program needn't handle non-finite values. No bound on the sum of `pair_mask` on one device may be relied on, other than what follows from the above.
Results may differ from the reference program's by a relative error of at most 0.007.
Values may be sent and summed in bfloat16 or wider, within the bound.
A program may use at most 128 MiB of HBM per device.

```python
import jax
import jax.numpy as jnp
from jax import lax

PAIR = 128
CHAINS = 4
RESIDUES = 80


def draw_chain_index(key, part):
    key = jax.random.fold_in(key, 11)
    order = jax.random.permutation(key, RESIDUES - 1).astype(jnp.int32)
    cuts = order[:CHAINS - 1] + 1
    position = jnp.arange(RESIDUES, dtype=jnp.int32)
    return jnp.sum((position[:, None] >= cuts[None, :]).astype(jnp.int32), axis=1).astype(jnp.int32)


def place_ends(values, own_key, smallest, high):
    longest = values.shape.index(max(values.shape))
    spots = []
    for shift in (0, 1):
        where = [jax.random.randint(jax.random.fold_in(own_key, axis), (), 0, length) for axis, length in enumerate(values.shape)]
        where[longest] = (where[longest] + shift) % values.shape[longest]
        spots.append(tuple(where))
    return values.at[spots[0]].set(smallest).at[spots[1]].set(high)


def level_of(rng, shape, split, low, high):
    factor_of, own = 1.0, jax.random.fold_in(rng, 6)
    for dim, blocks in split:
        steps = jnp.exp(jax.random.uniform(jax.random.fold_in(own, dim), (blocks,), jnp.float32, low / len(split), high / len(split)))
        factor_of = factor_of * jnp.repeat(steps, shape[dim] // blocks).reshape([-1 if axis == dim else 1 for axis in range(len(shape))])
    return factor_of


def gaussian(key, extent, spread, bound, shards=(), held_as=jnp.bfloat16):
    result = jax.random.normal(key, extent, jnp.float32) * spread
    if len(shards) > 0:
        result = level_of(key, extent, shards, -0.22, 0.18) * result
    return jnp.clip(result, min=-bound, max=bound).astype(held_as)


def setup_inputs(seed: int = 0, part: int = 0) -> dict:
    key_of = jax.random.split(jax.random.key(seed), 10)
    part_keys = jax.random.split(jax.random.fold_in(key_of[9], part), 10)
    pair_state = gaussian(part_keys[0], (RESIDUES, RESIDUES, PAIR), 1.0, 6.0, ((0, 16),))
    chain_index = draw_chain_index(jax.random.fold_in(jax.random.fold_in(key_of[9], part), 71), part)
    pair_mask = place_ends((jax.random.randint(part_keys[2], (RESIDUES, RESIDUES), 0, 10) < 9).astype(jnp.int32), jax.random.fold_in(part_keys[2], 1), 0, 1)
    chain_table = gaussian(key_of[3], (2, PAIR), 1.0, 4.0, (), jnp.float32)
    norm_gain = jnp.clip(1.0 + 0.18 * jax.random.normal(key_of[4], (2, 2, PAIR), jnp.float32), 0.1, 1.9)
    norm_shift = gaussian(key_of[5], (2, 2, PAIR), 0.5, 3.0, (), jnp.float32)
    projections = gaussian(key_of[6], (2, 5, PAIR, PAIR), PAIR ** -0.5, 0.5)
    output_weight = gaussian(key_of[7], (2, PAIR, PAIR), PAIR ** -0.5, 0.5)
    cotangent = gaussian(part_keys[8], (RESIDUES, RESIDUES, PAIR), 1.0, 6.0, ((0, 16),))
    return dict(pair_state=pair_state, chain_index=chain_index, pair_mask=pair_mask, chain_table=chain_table, norm_gain=norm_gain, norm_shift=norm_shift, projections=projections, output_weight=output_weight, cotangent=cotangent)


EPSILON = 1e-05

def normalize(values, norm_gain, norm_shift):
    center = values - lax.optimization_barrier(jnp.mean(values, axis=-1, keepdims=True))
    inverse = lax.rsqrt(lax.optimization_barrier(jnp.mean(center * center, axis=-1, keepdims=True)) + EPSILON)
    normed = center * inverse
    return (normed, inverse, normed * norm_gain + norm_shift)

def normalize_back(grad_output, normed, inverse, norm_gain):
    scaled = grad_output * norm_gain
    centered = scaled - lax.optimization_barrier(jnp.mean(scaled, axis=-1, keepdims=True))
    return (centered - normed * lax.optimization_barrier(jnp.mean(scaled * normed, axis=-1, keepdims=True))) * inverse

def block_forward(stream, masked, norm_gains, norm_shifts, weights, out_weight, incoming):
    channels = stream.shape[-1]
    normed_in, inverse_in, scaled_in = normalize(stream, norm_gains[0], norm_shifts[0])
    activated = scaled_in.astype(jnp.bfloat16)
    flattened = activated.reshape(-1, channels)
    projected = [jnp.dot(flattened, weights[number], preferred_element_type=jnp.float32).reshape(stream.shape) for number in range(5)]
    gate_left = jax.nn.sigmoid(projected[1])
    gate_right = jax.nn.sigmoid(projected[3])
    left_factor = (masked * gate_left * projected[0]).astype(jnp.bfloat16)
    right_factor = (masked * gate_right * projected[2]).astype(jnp.bfloat16)
    left_wide = left_factor.astype(jnp.float32)
    right_wide = right_factor.astype(jnp.float32)
    if incoming:
        product = jnp.einsum('kic,kjc->ijc', left_wide, right_wide)
    else:
        product = jnp.einsum('ikc,jkc->ijc', left_wide, right_wide)
    product = product.astype(jnp.bfloat16)
    normed_out, inverse_out, scaled_out = normalize(product.astype(jnp.float32), norm_gains[1], norm_shifts[1])
    mixture = scaled_out.astype(jnp.bfloat16)
    update = jnp.dot(mixture.reshape(-1, channels), out_weight, preferred_element_type=jnp.float32).reshape(stream.shape)
    out_gate = jax.nn.sigmoid(projected[4])
    following = (stream + out_gate * update).astype(jnp.bfloat16)
    stored = (activated, projected, left_wide, right_wide, normed_out, inverse_out, mixture, update, out_gate, normed_in, inverse_in)
    return (following, stored)

def block_backward(upstream, stored, masked, norm_gains, weights, out_weight, incoming):
    activated, projected, left_wide, right_wide, normed_out, inverse_out, mixture, update, out_gate, normed_in, inverse_in = stored
    channels = upstream.shape[-1]
    shape_full = upstream.shape
    update_grad = (upstream * out_gate).astype(jnp.bfloat16)
    gate_grad = upstream * update * out_gate * (1.0 - out_gate)
    out_weight_grad = jnp.dot(mixture.reshape(-1, channels).T, update_grad.reshape(-1, channels), preferred_element_type=jnp.float32) / RESIDUES
    mixture_grad = jnp.dot(update_grad.reshape(-1, channels), out_weight.T, preferred_element_type=jnp.float32).reshape(shape_full)
    product_grad = normalize_back(mixture_grad, normed_out, inverse_out, norm_gains[1]).astype(jnp.bfloat16)
    grad_wide = product_grad.astype(jnp.float32)
    if incoming:
        left_grad = jnp.einsum('ijc,kjc->kic', grad_wide, right_wide)
        right_grad = jnp.einsum('ijc,kic->kjc', grad_wide, left_wide)
    else:
        left_grad = jnp.einsum('ijc,jkc->ikc', grad_wide, right_wide)
        right_grad = jnp.einsum('ijc,ikc->jkc', grad_wide, left_wide)
    left_grad = left_grad.astype(jnp.bfloat16).astype(jnp.float32)
    right_grad = right_grad.astype(jnp.bfloat16).astype(jnp.float32)
    gate_left = jax.nn.sigmoid(projected[1])
    gate_right = jax.nn.sigmoid(projected[3])
    raw_grads = [left_grad * masked * gate_left, left_grad * masked * projected[0] * gate_left * (1.0 - gate_left), right_grad * masked * gate_right, right_grad * masked * projected[2] * gate_right * (1.0 - gate_right), gate_grad]
    flattened = activated.reshape(-1, channels)
    rounded = [element.astype(jnp.bfloat16).reshape(-1, channels) for element in raw_grads]
    weight_grads = jnp.stack([jnp.dot(flattened.T, element, preferred_element_type=jnp.float32) for element in rounded]) / RESIDUES
    input_grad = jnp.dot(rounded[0], weights[0].T, preferred_element_type=jnp.float32)
    for number in range(1, 5):
        input_grad = input_grad + jnp.dot(rounded[number], weights[number].T, preferred_element_type=jnp.float32)
    input_grad = input_grad.reshape(shape_full)
    stream_grad = upstream + normalize_back(input_grad, normed_in, inverse_in, norm_gains[0])
    return (stream_grad, weight_grads, out_weight_grad)

def reference(pair_state, chain_index, pair_mask, chain_table, norm_gain, norm_shift, projections, output_weight, cotangent):
    same_chain = chain_index[:, None] == chain_index[None, :]
    stream = pair_state.astype(jnp.float32) + jnp.where(same_chain[:, :, None], chain_table[1], chain_table[0])
    masked = pair_mask.astype(jnp.float32)[:, :, None]
    following, stored_first = block_forward(stream, masked, norm_gain[0], norm_shift[0], projections[0], output_weight[0], False)
    ignored, stored_second = block_forward(following.astype(jnp.float32), masked, norm_gain[1], norm_shift[1], projections[1], output_weight[1], True)
    grad_mid, proj_second, out_second = block_backward(cotangent.astype(jnp.float32), stored_second, masked, norm_gain[1], projections[1], output_weight[1], True)
    grad_first, proj_first, out_first = block_backward(grad_mid, stored_first, masked, norm_gain[0], projections[0], output_weight[0], False)
    return (grad_first.astype(jnp.bfloat16), jnp.stack([proj_first, proj_second]), jnp.stack([out_first, out_second]))
```

```python
import functools

import jax
import jax.numpy as jnp
from jax import lax
from jax.experimental import pallas as pl
from jax.experimental.pallas import tpu as pltpu
from jax.sharding import PartitionSpec as P

EPSILON = 1e-05


def normalize(values, norm_gain, norm_shift, reduce_axis):
    center = values - jnp.mean(values, axis=reduce_axis, keepdims=True)
    inverse = lax.rsqrt(jnp.mean(center * center, axis=reduce_axis, keepdims=True) + EPSILON)
    normed = center * inverse
    return (normed, inverse, normed * norm_gain + norm_shift)


def normalize_back(grad_output, normed, inverse, norm_gain, reduce_axis):
    scaled = grad_output * norm_gain
    centered = scaled - jnp.mean(scaled, axis=reduce_axis, keepdims=True)
    return (
        centered - normed * jnp.mean(scaled * normed, axis=reduce_axis, keepdims=True)
    ) * inverse


def multiply(left_cols, right_cols, incoming):
    if incoming:
        return jnp.einsum(
            "xcki,xckj->xcij", left_cols, right_cols, preferred_element_type=jnp.float32
        )
    return jnp.einsum("xcik,xcjk->xcij", left_cols, right_cols, preferred_element_type=jnp.float32)


def factor_grads(grad_cols, left_cols, right_cols, incoming):
    if incoming:
        left_grad = jnp.einsum(
            "xcij,xckj->xcki", grad_cols, right_cols, preferred_element_type=jnp.float32
        )
        right_grad = jnp.einsum(
            "xcij,xcki->xckj", grad_cols, left_cols, preferred_element_type=jnp.float32
        )
    else:
        left_grad = jnp.einsum(
            "xcij,xcjk->xcik", grad_cols, right_cols, preferred_element_type=jnp.float32
        )
        right_grad = jnp.einsum(
            "xcij,xcik->xcjk", grad_cols, left_cols, preferred_element_type=jnp.float32
        )
    return (left_grad.astype(jnp.bfloat16), right_grad.astype(jnp.bfloat16))


def block_forward(stream, masked, norm_gains, norm_shifts, weights, out_weight, incoming):
    rows, residues, channels = stream.shape
    devices = lax.axis_size("dap")
    slices = channels // devices
    normed_in, inverse_in, scaled_in = normalize(stream, norm_gains[0], norm_shifts[0], 2)
    activated = scaled_in.astype(jnp.bfloat16)
    factor_pre = jnp.einsum(
        "rnd,pdc->pcrn", activated, weights[:4], preferred_element_type=jnp.float32
    )
    gate_pre = jnp.einsum("rnd,dc->rnc", activated, weights[4], preferred_element_type=jnp.float32)
    gate_left = jax.nn.sigmoid(factor_pre[1])
    gate_right = jax.nn.sigmoid(factor_pre[3])
    left_factor = (masked * gate_left * factor_pre[0]).astype(jnp.bfloat16)
    right_factor = (masked * gate_right * factor_pre[2]).astype(jnp.bfloat16)
    left_blocks = left_factor.reshape(devices, slices, rows, residues)
    right_blocks = right_factor.reshape(devices, slices, rows, residues)
    left_cols, right_cols = (
        lax.all_to_all(left_blocks, "dap", split_axis=0, concat_axis=2, tiled=True),
        lax.all_to_all(right_blocks, "dap", split_axis=0, concat_axis=2, tiled=True),
    )
    product = multiply(left_cols, right_cols, incoming).astype(jnp.bfloat16)
    returned = lax.all_to_all(product, "dap", split_axis=2, concat_axis=0, tiled=True)
    product_rows = returned.reshape(channels, rows, residues)
    normed_out, inverse_out, scaled_out = normalize(
        product_rows.astype(jnp.float32),
        norm_gains[1][:, None, None],
        norm_shifts[1][:, None, None],
        0,
    )
    mixture = scaled_out.astype(jnp.bfloat16)
    update = jnp.einsum("crn,cd->rnd", mixture, out_weight, preferred_element_type=jnp.float32)
    out_gate = jax.nn.sigmoid(gate_pre)
    following = (stream + out_gate * update).astype(jnp.bfloat16)
    stored = (
        activated,
        factor_pre,
        left_cols,
        right_cols,
        normed_out,
        inverse_out,
        mixture,
        update,
        out_gate,
        normed_in,
        inverse_in,
    )
    return (following, stored)


def block_backward(upstream, stored, masked, norm_gains, weights, out_weight, incoming):
    (
        activated,
        factor_pre,
        left_cols,
        right_cols,
        normed_out,
        inverse_out,
        mixture,
        update,
        out_gate,
        normed_in,
        inverse_in,
    ) = stored
    rows, residues, channels = upstream.shape
    devices = lax.axis_size("dap")
    slices = channels // devices
    update_grad = (upstream * out_gate).astype(jnp.bfloat16)
    gate_grad = (upstream * update * out_gate * (1.0 - out_gate)).astype(jnp.bfloat16)
    out_weight_grad = jnp.einsum(
        "crn,rnd->cd", mixture, update_grad, preferred_element_type=jnp.float32
    )
    mixture_grad = jnp.einsum(
        "rnd,cd->crn", update_grad, out_weight, preferred_element_type=jnp.float32
    )
    product_grad = normalize_back(
        mixture_grad, normed_out, inverse_out, norm_gains[1][:, None, None], 0
    ).astype(jnp.bfloat16)
    grad_blocks = product_grad.reshape(devices, slices, rows, residues)
    grad_cols = lax.all_to_all(grad_blocks, "dap", split_axis=0, concat_axis=2, tiled=True)
    left_grad, right_grad = factor_grads(grad_cols, left_cols, right_cols, incoming)
    left_back, right_back = (
        lax.all_to_all(left_grad, "dap", split_axis=2, concat_axis=0, tiled=True),
        lax.all_to_all(right_grad, "dap", split_axis=2, concat_axis=0, tiled=True),
    )
    left_rows = left_back.reshape(channels, rows, residues).astype(jnp.float32)
    right_rows = right_back.reshape(channels, rows, residues).astype(jnp.float32)
    gate_left = jax.nn.sigmoid(factor_pre[1])
    gate_right = jax.nn.sigmoid(factor_pre[3])
    factor_grad = jnp.stack(
        [
            left_rows * masked * gate_left,
            left_rows * masked * factor_pre[0] * gate_left * (1.0 - gate_left),
            right_rows * masked * gate_right,
            right_rows * masked * factor_pre[2] * gate_right * (1.0 - gate_right),
        ]
    ).astype(jnp.bfloat16)
    factor_weight_grads = jnp.einsum(
        "rnd,pcrn->pdc", activated, factor_grad, preferred_element_type=jnp.float32
    )
    gate_weight_grad = jnp.einsum(
        "rnd,rnc->dc", activated, gate_grad, preferred_element_type=jnp.float32
    )
    weight_grads = jnp.concatenate([factor_weight_grads, gate_weight_grad[None]], 0)
    input_grad = jnp.einsum(
        "pcrn,pdc->rnd", factor_grad, weights[:4], preferred_element_type=jnp.float32
    )
    input_grad = input_grad + jnp.einsum(
        "rnc,dc->rnd", gate_grad, weights[4], preferred_element_type=jnp.float32
    )
    stream_grad = upstream + normalize_back(input_grad, normed_in, inverse_in, norm_gains[0], 2)
    return (stream_grad, weight_grads, out_weight_grad)


def reduce_block(weight_grads, out_weight_grad):
    return lax.psum((weight_grads, out_weight_grad), "dap")


def sharded_ops(
    pair_state,
    chain_index,
    pair_mask,
    chain_table,
    norm_gain,
    norm_shift,
    projections,
    output_weight,
    cotangent,
):
    rows, residues, channels = pair_state.shape
    first_row = lax.axis_index("dap") * rows
    own_chain = lax.dynamic_slice_in_dim(chain_index, first_row, rows, 0)
    same_chain = own_chain[:, None] == chain_index[None, :]
    stream = pair_state.astype(jnp.float32) + jnp.where(
        same_chain[:, :, None], chain_table[1], chain_table[0]
    )
    masked = pair_mask.astype(jnp.float32)[None]
    following, stored_first = block_forward(
        stream, masked, norm_gain[0], norm_shift[0], projections[0], output_weight[0], False
    )
    ignored, stored_second = block_forward(
        following.astype(jnp.float32),
        masked,
        norm_gain[1],
        norm_shift[1],
        projections[1],
        output_weight[1],
        True,
    )
    grad_mid, proj_second, out_second = block_backward(
        cotangent.astype(jnp.float32),
        stored_second,
        masked,
        norm_gain[1],
        projections[1],
        output_weight[1],
        True,
    )
    proj_second, out_second = reduce_block(proj_second, out_second)
    grad_first, proj_first, out_first = block_backward(
        grad_mid, stored_first, masked, norm_gain[0], projections[0], output_weight[0], False
    )
    proj_first, out_first = reduce_block(proj_first, out_first)
    scale_rows = 1.0 / residues
    projection_grads = jnp.stack([proj_first, proj_second]) * scale_rows
    weight_grad_out = jnp.stack([out_first, out_second]) * scale_rows
    return (grad_first.astype(jnp.bfloat16), projection_grads, weight_grad_out)


LANES = 128
F32 = jnp.float32
BF16 = jnp.bfloat16


def dot(left, right, left_dim, right_dim):
    return lax.dot_general(
        left, right, (((left_dim,), (right_dim,)), ((), ())), preferred_element_type=F32
    )


def norm_lanes(values):
    center = values - jnp.mean(values, axis=1, keepdims=True)
    inverse = lax.rsqrt(jnp.mean(center * center, axis=1, keepdims=True) + EPSILON)
    return center * inverse, inverse


def norm_lanes_back(grad, normed, inverse, gain):
    scaled = grad * gain
    centered = scaled - jnp.mean(scaled, axis=1, keepdims=True)
    return (centered - normed * jnp.mean(scaled * normed, axis=1, keepdims=True)) * inverse


def fused_kernel(
    n,
    rows,
    residues,
    pair_ref,
    chain_ref,
    mask_ref,
    table_ref,
    gain_ref,
    shift_ref,
    proj_ref,
    weight_ref,
    cot_ref,
    grad_out,
    proj_out,
    weight_out,
    stream,
    mask,
    normed_in,
    inverse_in,
    normed_out,
    inverse_out,
    activated,
    pre,
    mixture,
    update,
    up,
    mix_grad,
    update_grad,
    pre_grad,
    factors,
    stage16,
    stage8,
    rows16,
    rows8,
    wide_send,
    wide_recv,
    thin_send,
    thin_recv,
    sum_send,
    sum_recv,
    all_send,
    all_recv,
    total,
    send_sem,
    recv_sem,
):
    channels = LANES
    slices = channels // n
    padded = factors.shape[-1]
    pairs = rows * residues
    share = sum_recv.shape[2]
    double = 2 * slices
    me = lax.axis_index("dap")
    barrier = pltpu.get_barrier_semaphore()

    def each_peer(body):
        def step(index, carry):
            body(lax.rem(me + index, n))
            return carry

        lax.fori_loop(1, n, step, 0)

    def greet(peer):
        pl.semaphore_signal(
            barrier, inc=1, device_id={"dap": peer}, device_id_type=pl.DeviceIdType.MESH
        )

    each_peer(greet)

    def copy(phase, source, target, peer, owner):
        return pltpu.make_async_remote_copy(
            src_ref=source,
            dst_ref=target.at[owner],
            send_sem=send_sem.at[phase, peer],
            recv_sem=recv_sem.at[phase, owner],
            device_id={"dap": peer},
            device_id_type=pl.DeviceIdType.MESH,
        )

    def send_all(phase, source_of, target):
        target[me] = source_of(me)[...]
        each_peer(lambda peer: copy(phase, source_of(peer), target, peer, me).start())

    def take_all(phase, source_of, target):
        each_peer(lambda peer: copy(phase, source_of(peer), target, peer, peer).wait_recv())

    def end_all(phase, source_of, target):
        each_peer(lambda peer: copy(phase, source_of(peer), target, peer, me).wait_send())

    def span(row):
        return pl.ds(row * residues, residues)

    def to_columns(values):
        filler = jnp.zeros((padded - residues, channels), F32)
        full = jnp.concatenate([values, filler], axis=0) if padded > residues else values
        return full.T.reshape(n, slices, padded)

    def to_rows(blocks):
        return blocks.reshape(channels, padded).T[:residues]

    def wide(number):
        return lambda peer: wide_send.at[number, peer]

    def thin(number):
        return lambda peer: thin_send.at[number, peer]

    def shares(number):
        return lambda peer: sum_send.at[
            number, pl.ds(pl.multiple_of(peer * share, 16), share)
        ]

    def whole_share(number):
        return lambda peer: all_send.at[number]

    exchanges = {
        0: (wide(0), wide_recv.at[0]),
        1: (thin(0), thin_recv.at[0]),
        2: (wide(1), wide_recv.at[1]),
        3: (thin(1), thin_recv.at[1]),
        4: (thin(2), thin_recv.at[2]),
        5: (wide(2), wide_recv.at[2]),
        6: (thin(3), thin_recv.at[3]),
        7: (wide(3), wide_recv.at[3]),
        8: (shares(1), sum_recv.at[1]),
        9: (whole_share(1), all_recv.at[1]),
        10: (shares(0), sum_recv.at[0]),
        11: (whole_share(0), all_recv.at[0]),
    }

    stage16[...] = jnp.zeros_like(stage16)
    stage8[...] = jnp.zeros_like(stage8)
    rows8[...] = jnp.zeros_like(rows8)

    chain = chain_ref[...]
    place = lax.broadcasted_iota(jnp.int32, chain.shape, 1)
    for row in range(rows):
        own = jnp.sum(jnp.where(place == me * rows + row, chain, 0), axis=1, keepdims=True)
        same = jnp.where(chain == own, 1.0, 0.0).astype(F32)
        filler = jnp.zeros((1, padded - residues), F32)
        seen = mask_ref[pl.ds(row, 1), :].astype(F32)
        if padded > residues:
            same = jnp.concatenate([same, filler], axis=1)
            seen = jnp.concatenate([seen, filler], axis=1)
        same = jnp.broadcast_to(same, (channels, padded)).T[:residues]
        mask[span(row), :] = jnp.broadcast_to(seen, (channels, padded)).T[:residues]
        stream[0, span(row), :] = pair_ref[row].astype(F32) + jnp.where(
            same > 0.5, table_ref[1:2, :], table_ref[0:1, :]
        )

    def send_factors(number):
        gain, shift = gain_ref[number, 0:1, :], shift_ref[number, 0:1, :]
        for row in range(rows):
            normed, inverse = norm_lanes(stream[number, span(row), :])
            normed_in[number, span(row), :] = normed
            inverse_in[number, span(row), :] = jnp.broadcast_to(inverse, normed.shape)
            activated[number, span(row), :] = (normed * gain + shift).astype(BF16)
        for part in range(5):
            pre[number, part] = dot(activated[number], proj_ref[number, part], 1, 0)
        for row in range(rows):
            seen = mask[span(row), :]
            left = seen * jax.nn.sigmoid(pre[number, 1, span(row)]) * pre[number, 0, span(row)]
            right = seen * jax.nn.sigmoid(pre[number, 3, span(row)]) * pre[number, 2, span(row)]
            both = jnp.concatenate([to_columns(left), to_columns(right)], axis=1)
            wide_send[number, :, pl.ds(row * double, double), :] = both.astype(BF16)
        if number == 0:
            pl.semaphore_wait(barrier, n - 1)
        send_all(2 * number, *exchanges[2 * number])

    def send_product(number):
        take_all(2 * number, *exchanges[2 * number])
        for owner in range(n):
            stage16[pl.ds(owner * rows * double, rows * double), :] = wide_recv[
                number, owner
            ].astype(F32)
        for channel in range(slices):
            left = stage16[pl.ds(channel, padded, stride=double), :].astype(BF16)
            right = stage16[pl.ds(slices + channel, padded, stride=double), :].astype(BF16)
            factors[number, 0, channel] = left
            factors[number, 1, channel] = right
            stage8[pl.ds(channel, padded, stride=slices), :] = dot(
                left, right, 1 - number, 1 - number
            )
        thin_rows = thin_send.shape[2]
        for owner in range(n):
            thin_send[number, owner] = stage8[
                pl.ds(owner * rows * slices, thin_rows), :
            ].astype(BF16)
        send_all(2 * number + 1, *exchanges[2 * number + 1])

    def take_product(number):
        take_all(2 * number + 1, *exchanges[2 * number + 1])
        gain, shift = gain_ref[number, 1:2, :], shift_ref[number, 1:2, :]
        rows8[...] = thin_recv[number].astype(F32)
        for row in range(rows):
            product = to_rows(rows8[:, pl.ds(row * slices, slices), :])
            normed, inverse = norm_lanes(product)
            normed_out[number, span(row), :] = normed
            inverse_out[number, span(row), :] = jnp.broadcast_to(inverse, normed.shape)
            mixture[number, span(row), :] = (normed * gain + shift).astype(BF16)

    def take_update(number):
        update[number] = dot(mixture[number], weight_ref[number], 1, 0)

    def mixture_back(number):
        for row in range(rows):
            gate = jax.nn.sigmoid(pre[number, 4, span(row)])
            update_grad[number, span(row), :] = (up[number, span(row)] * gate).astype(BF16)
        mix_grad[...] = dot(update_grad[number], weight_ref[number], 1, 1)

    def send_product_grad(number):
        gain = gain_ref[number, 1:2, :]
        for row in range(rows):
            grad = norm_lanes_back(
                mix_grad[span(row), :],
                normed_out[number, span(row), :],
                inverse_out[number, span(row), :],
                gain,
            )
            rows8[:, pl.ds(row * slices, slices), :] = to_columns(grad)
        thin_send[3 - number] = rows8[...].astype(BF16)
        send_all(6 - 2 * number, *exchanges[6 - 2 * number])

    def gate_back(number):
        for row in range(rows):
            gate = jax.nn.sigmoid(pre[number, 4, span(row)])
            pre_grad[number, 4, span(row), :] = (
                up[number, span(row)] * update[number, span(row)] * gate * (1.0 - gate)
            ).astype(BF16)

    def weight_sum(number, part):
        if part == 5:
            grad = dot(mixture[number], update_grad[number], 0, 0)
        else:
            grad = dot(activated[number], pre_grad[number, part], 0, 0)
        sum_send[number, pl.ds(part * channels, channels), :] = (
            grad * (1.0 / residues)
        ).astype(BF16)

    def send_factor_grads(number):
        phase = 6 - 2 * number
        take_all(phase, *exchanges[phase])
        for owner in range(n):
            block = thin_recv[3 - number, owner].astype(F32)
            stage8[pl.ds(owner * rows * slices, rows * slices), :] = block[: rows * slices]
        if padded > residues:
            stage8[pl.ds(residues * slices, (padded - residues) * slices), :] = jnp.zeros(
                ((padded - residues) * slices, padded), F32
            )
        for channel in range(slices):
            grad = stage8[pl.ds(channel, padded, stride=slices), :].astype(BF16)
            left, right = factors[number, 0, channel], factors[number, 1, channel]
            if number == 0:
                left_grad = dot(grad, right, 1, 0)
                right_grad = dot(grad, left, 0, 0)
            else:
                left_grad = dot(right, grad, 1, 1)
                right_grad = dot(left, grad, 1, 0)
            stage16[pl.ds(channel, padded, stride=double), :] = left_grad
            stage16[pl.ds(slices + channel, padded, stride=double), :] = right_grad
        for owner in range(n):
            wide_send[3 - number, owner] = stage16[
                pl.ds(owner * rows * double, rows * double), :
            ].astype(BF16)
        send_all(phase + 1, *exchanges[phase + 1])

    def take_factor_grads(number):
        phase = 7 - 2 * number
        take_all(phase, *exchanges[phase])
        rows16[...] = wide_recv[3 - number].astype(F32)
        for row in range(rows):
            seen = mask[span(row), :]
            for side in range(2):
                grad = seen * to_rows(rows16[:, pl.ds(row * double + side * slices, slices), :])
                gate = jax.nn.sigmoid(pre[number, 2 * side + 1, span(row)])
                opened = grad * gate
                pre_grad[number, 2 * side, span(row), :] = opened.astype(BF16)
                pre_grad[number, 2 * side + 1, span(row), :] = (
                    opened * pre[number, 2 * side, span(row)] * (1.0 - gate)
                ).astype(BF16)

    def stream_back(number):
        inner = dot(pre_grad[number, 0], proj_ref[number, 0], 1, 1)
        for part in range(1, 5):
            inner = inner + dot(pre_grad[number, part], proj_ref[number, part], 1, 1)
        mix_grad[...] = inner
        gain = gain_ref[number, 0:1, :]
        for row in range(rows):
            grad = up[number, span(row)] + norm_lanes_back(
                mix_grad[span(row), :],
                normed_in[number, span(row), :],
                inverse_in[number, span(row), :],
                gain,
            )
            if number == 1:
                up[0, span(row), :] = grad
            else:
                grad_out[row] = grad.astype(BF16)

    def send_total(number):
        phase = 10 - 2 * number
        take_all(phase, *exchanges[phase])
        result = sum_recv[number, 0].astype(F32)
        for owner in range(1, n):
            result = result + sum_recv[number, owner].astype(F32)
        all_send[number] = result.astype(BF16)
        send_all(phase + 1, *exchanges[phase + 1])

    def take_total(number):
        phase = 11 - 2 * number
        take_all(phase, *exchanges[phase])
        for owner in range(n):
            total[pl.ds(owner * share, share), :] = all_recv[number, owner].astype(F32)
        for part in range(5):
            proj_out[number, part] = total[pl.ds(part * channels, channels), :]
        weight_out[number] = total[pl.ds(5 * channels, channels), :]

    send_factors(0)
    up[1] = cot_ref[...].reshape(pairs, channels).astype(F32)
    send_product(0)
    take_product(0)
    take_update(0)
    for row in range(rows):
        gate = jax.nn.sigmoid(pre[0, 4, span(row)])
        stream[1, span(row), :] = (
            (stream[0, span(row), :] + gate * update[0, span(row)]).astype(BF16).astype(F32)
        )
    send_factors(1)
    mixture_back(1)
    send_product(1)
    take_product(1)
    send_product_grad(1)
    take_update(1)
    gate_back(1)
    send_factor_grads(1)
    weight_sum(1, 4)
    weight_sum(1, 5)
    take_factor_grads(1)
    stream_back(1)
    mixture_back(0)
    send_product_grad(0)
    for part in range(4):
        weight_sum(1, part)
    send_all(8, *exchanges[8])
    gate_back(0)
    send_factor_grads(0)
    weight_sum(0, 4)
    weight_sum(0, 5)
    send_total(1)
    take_factor_grads(0)
    for part in range(4):
        weight_sum(0, part)
    send_all(10, *exchanges[10])
    stream_back(0)
    take_total(1)
    send_total(0)
    take_total(0)
    for phase in range(12):
        end_all(phase, *exchanges[phase])


def fused(
    pair_state,
    chain_index,
    pair_mask,
    chain_table,
    norm_gain,
    norm_shift,
    projections,
    output_weight,
    cotangent,
):
    rows, residues, channels = pair_state.shape
    n = lax.axis_size("dap")
    slices = channels // n
    padded = -(-residues // LANES) * LANES
    pairs = rows * residues
    double = rows * 2 * slices
    single = -(-rows * slices // 16) * 16
    share = 6 * channels // n
    vmem = pl.BlockSpec(memory_space=pltpu.VMEM)
    return pl.pallas_call(
        functools.partial(fused_kernel, n, rows, residues),
        out_shape=(
            jax.ShapeDtypeStruct((rows, residues, channels), BF16),
            jax.ShapeDtypeStruct((2, 5, channels, channels), F32),
            jax.ShapeDtypeStruct((2, channels, channels), F32),
        ),
        in_specs=[vmem] * 9,
        out_specs=(vmem,) * 3,
        scratch_shapes=[
            pltpu.VMEM((2, pairs, channels), F32),
            pltpu.VMEM((pairs, channels), F32),
            pltpu.VMEM((2, pairs, channels), F32),
            pltpu.VMEM((2, pairs, channels), F32),
            pltpu.VMEM((2, pairs, channels), F32),
            pltpu.VMEM((2, pairs, channels), F32),
            pltpu.VMEM((2, pairs, channels), BF16),
            pltpu.VMEM((2, 5, pairs, channels), F32),
            pltpu.VMEM((2, pairs, channels), BF16),
            pltpu.VMEM((2, pairs, channels), F32),
            pltpu.VMEM((2, pairs, channels), F32),
            pltpu.VMEM((pairs, channels), F32),
            pltpu.VMEM((2, pairs, channels), BF16),
            pltpu.VMEM((2, 5, pairs, channels), BF16),
            pltpu.VMEM((2, 2, slices, padded, padded), BF16),
            pltpu.VMEM((padded * 2 * slices, padded), F32),
            pltpu.VMEM((padded * slices, padded), F32),
            pltpu.VMEM((n, double, padded), F32),
            pltpu.VMEM((n, single, padded), F32),
            pltpu.VMEM((4, n, double, padded), BF16),
            pltpu.VMEM((4, n, double, padded), BF16),
            pltpu.VMEM((4, n, single, padded), BF16),
            pltpu.VMEM((4, n, single, padded), BF16),
            pltpu.VMEM((2, 6 * channels, channels), BF16),
            pltpu.VMEM((2, n, share, channels), BF16),
            pltpu.VMEM((2, share, channels), BF16),
            pltpu.VMEM((2, n, share, channels), BF16),
            pltpu.VMEM((6 * channels, channels), F32),
            pltpu.SemaphoreType.DMA((12, n)),
            pltpu.SemaphoreType.DMA((12, n)),
        ],
        compiler_params=pltpu.CompilerParams(
            collective_id=0, has_side_effects=True, vmem_limit_bytes=40 * 2**20
        ),
    )(
        pair_state,
        chain_index.reshape(1, residues),
        pair_mask,
        chain_table,
        norm_gain,
        norm_shift,
        projections,
        output_weight,
        cotangent,
    )


def fits(rows, residues, channels, n):
    padded = -(-residues // LANES) * LANES
    return (
        channels == LANES
        and channels % n == 0
        and (channels // n) % 8 == 0
        and (6 * channels // n) % 16 == 0
        and residues % 16 == 0
        and padded <= 2 * LANES
        and padded - residues >= 2
    )


def shards(*arguments):
    rows, residues, channels = arguments[0].shape
    n = lax.axis_size("dap")
    if fits(rows, residues, channels, n):
        return fused(*arguments)
    return sharded_ops(*arguments)


def solution(mesh):
    return jax.shard_map(
        shards,
        mesh=mesh,
        in_specs=(
            P(("groups", "dap"), None, None),
            P("groups"),
            P(("groups", "dap"), None),
            P(),
            P(),
            P(),
            P(),
            P(),
            P(("groups", "dap"), None, None),
        ),
        out_specs=(
            P(("groups", "dap"), None, None),
            P("groups", None, None, None),
            P("groups", None, None),
        ),
        check_vma=False,
    )
```

```python
import functools

import jax
import jax.numpy as jnp
from jax import lax
from jax.experimental import pallas as pl
from jax.experimental.pallas import tpu as pltpu
from jax.sharding import PartitionSpec as P

EPSILON = 1e-05


def normalize(values, norm_gain, norm_shift, reduce_axis):
    center = values - jnp.mean(values, axis=reduce_axis, keepdims=True)
    inverse = lax.rsqrt(jnp.mean(center * center, axis=reduce_axis, keepdims=True) + EPSILON)
    normed = center * inverse
    return (normed, inverse, normed * norm_gain + norm_shift)


def normalize_back(grad_output, normed, inverse, norm_gain, reduce_axis):
    scaled = grad_output * norm_gain
    centered = scaled - jnp.mean(scaled, axis=reduce_axis, keepdims=True)
    return (
        centered - normed * jnp.mean(scaled * normed, axis=reduce_axis, keepdims=True)
    ) * inverse


def multiply(left_cols, right_cols, incoming):
    if incoming:
        return jnp.einsum(
            "xcki,xckj->xcij", left_cols, right_cols, preferred_element_type=jnp.float32
        )
    return jnp.einsum("xcik,xcjk->xcij", left_cols, right_cols, preferred_element_type=jnp.float32)


def factor_grads(grad_cols, left_cols, right_cols, incoming):
    if incoming:
        left_grad = jnp.einsum(
            "xcij,xckj->xcki", grad_cols, right_cols, preferred_element_type=jnp.float32
        )
        right_grad = jnp.einsum(
            "xcij,xcki->xckj", grad_cols, left_cols, preferred_element_type=jnp.float32
        )
    else:
        left_grad = jnp.einsum(
            "xcij,xcjk->xcik", grad_cols, right_cols, preferred_element_type=jnp.float32
        )
        right_grad = jnp.einsum(
            "xcij,xcik->xcjk", grad_cols, left_cols, preferred_element_type=jnp.float32
        )
    return (left_grad.astype(jnp.bfloat16), right_grad.astype(jnp.bfloat16))


def block_forward(stream, masked, norm_gains, norm_shifts, weights, out_weight, incoming):
    rows, residues, channels = stream.shape
    devices = lax.axis_size("dap")
    slices = channels // devices
    normed_in, inverse_in, scaled_in = normalize(stream, norm_gains[0], norm_shifts[0], 2)
    activated = scaled_in.astype(jnp.bfloat16)
    factor_pre = jnp.einsum(
        "rnd,pdc->pcrn", activated, weights[:4], preferred_element_type=jnp.float32
    )
    gate_pre = jnp.einsum("rnd,dc->rnc", activated, weights[4], preferred_element_type=jnp.float32)
    gate_left = jax.nn.sigmoid(factor_pre[1])
    gate_right = jax.nn.sigmoid(factor_pre[3])
    left_factor = (masked * gate_left * factor_pre[0]).astype(jnp.bfloat16)
    right_factor = (masked * gate_right * factor_pre[2]).astype(jnp.bfloat16)
    left_blocks = left_factor.reshape(devices, slices, rows, residues)
    right_blocks = right_factor.reshape(devices, slices, rows, residues)
    left_cols, right_cols = (
        lax.all_to_all(left_blocks, "dap", split_axis=0, concat_axis=2, tiled=True),
        lax.all_to_all(right_blocks, "dap", split_axis=0, concat_axis=2, tiled=True),
    )
    product = multiply(left_cols, right_cols, incoming).astype(jnp.bfloat16)
    returned = lax.all_to_all(product, "dap", split_axis=2, concat_axis=0, tiled=True)
    product_rows = returned.reshape(channels, rows, residues)
    normed_out, inverse_out, scaled_out = normalize(
        product_rows.astype(jnp.float32),
        norm_gains[1][:, None, None],
        norm_shifts[1][:, None, None],
        0,
    )
    mixture = scaled_out.astype(jnp.bfloat16)
    update = jnp.einsum("crn,cd->rnd", mixture, out_weight, preferred_element_type=jnp.float32)
    out_gate = jax.nn.sigmoid(gate_pre)
    following = (stream + out_gate * update).astype(jnp.bfloat16)
    stored = (
        activated,
        factor_pre,
        left_cols,
        right_cols,
        normed_out,
        inverse_out,
        mixture,
        update,
        out_gate,
        normed_in,
        inverse_in,
    )
    return (following, stored)


def block_backward(upstream, stored, masked, norm_gains, weights, out_weight, incoming):
    (
        activated,
        factor_pre,
        left_cols,
        right_cols,
        normed_out,
        inverse_out,
        mixture,
        update,
        out_gate,
        normed_in,
        inverse_in,
    ) = stored
    rows, residues, channels = upstream.shape
    devices = lax.axis_size("dap")
    slices = channels // devices
    update_grad = (upstream * out_gate).astype(jnp.bfloat16)
    gate_grad = (upstream * update * out_gate * (1.0 - out_gate)).astype(jnp.bfloat16)
    out_weight_grad = jnp.einsum(
        "crn,rnd->cd", mixture, update_grad, preferred_element_type=jnp.float32
    )
    mixture_grad = jnp.einsum(
        "rnd,cd->crn", update_grad, out_weight, preferred_element_type=jnp.float32
    )
    product_grad = normalize_back(
        mixture_grad, normed_out, inverse_out, norm_gains[1][:, None, None], 0
    ).astype(jnp.bfloat16)
    grad_blocks = product_grad.reshape(devices, slices, rows, residues)
    grad_cols = lax.all_to_all(grad_blocks, "dap", split_axis=0, concat_axis=2, tiled=True)
    left_grad, right_grad = factor_grads(grad_cols, left_cols, right_cols, incoming)
    left_back, right_back = (
        lax.all_to_all(left_grad, "dap", split_axis=2, concat_axis=0, tiled=True),
        lax.all_to_all(right_grad, "dap", split_axis=2, concat_axis=0, tiled=True),
    )
    left_rows = left_back.reshape(channels, rows, residues).astype(jnp.float32)
    right_rows = right_back.reshape(channels, rows, residues).astype(jnp.float32)
    gate_left = jax.nn.sigmoid(factor_pre[1])
    gate_right = jax.nn.sigmoid(factor_pre[3])
    factor_grad = jnp.stack(
        [
            left_rows * masked * gate_left,
            left_rows * masked * factor_pre[0] * gate_left * (1.0 - gate_left),
            right_rows * masked * gate_right,
            right_rows * masked * factor_pre[2] * gate_right * (1.0 - gate_right),
        ]
    ).astype(jnp.bfloat16)
    factor_weight_grads = jnp.einsum(
        "rnd,pcrn->pdc", activated, factor_grad, preferred_element_type=jnp.float32
    )
    gate_weight_grad = jnp.einsum(
        "rnd,rnc->dc", activated, gate_grad, preferred_element_type=jnp.float32
    )
    weight_grads = jnp.concatenate([factor_weight_grads, gate_weight_grad[None]], 0)
    input_grad = jnp.einsum(
        "pcrn,pdc->rnd", factor_grad, weights[:4], preferred_element_type=jnp.float32
    )
    input_grad = input_grad + jnp.einsum(
        "rnc,dc->rnd", gate_grad, weights[4], preferred_element_type=jnp.float32
    )
    stream_grad = upstream + normalize_back(input_grad, normed_in, inverse_in, norm_gains[0], 2)
    return (stream_grad, weight_grads, out_weight_grad)


def reduce_block(weight_grads, out_weight_grad):
    return lax.psum((weight_grads, out_weight_grad), "dap")


def sharded_ops(
    pair_state,
    chain_index,
    pair_mask,
    chain_table,
    norm_gain,
    norm_shift,
    projections,
    output_weight,
    cotangent,
):
    rows, residues, channels = pair_state.shape
    first_row = lax.axis_index("dap") * rows
    own_chain = lax.dynamic_slice_in_dim(chain_index, first_row, rows, 0)
    same_chain = own_chain[:, None] == chain_index[None, :]
    stream = pair_state.astype(jnp.float32) + jnp.where(
        same_chain[:, :, None], chain_table[1], chain_table[0]
    )
    masked = pair_mask.astype(jnp.float32)[None]
    following, stored_first = block_forward(
        stream, masked, norm_gain[0], norm_shift[0], projections[0], output_weight[0], False
    )
    ignored, stored_second = block_forward(
        following.astype(jnp.float32),
        masked,
        norm_gain[1],
        norm_shift[1],
        projections[1],
        output_weight[1],
        True,
    )
    grad_mid, proj_second, out_second = block_backward(
        cotangent.astype(jnp.float32),
        stored_second,
        masked,
        norm_gain[1],
        projections[1],
        output_weight[1],
        True,
    )
    proj_second, out_second = reduce_block(proj_second, out_second)
    grad_first, proj_first, out_first = block_backward(
        grad_mid, stored_first, masked, norm_gain[0], projections[0], output_weight[0], False
    )
    proj_first, out_first = reduce_block(proj_first, out_first)
    scale_rows = 1.0 / residues
    projection_grads = jnp.stack([proj_first, proj_second]) * scale_rows
    weight_grad_out = jnp.stack([out_first, out_second]) * scale_rows
    return (grad_first.astype(jnp.bfloat16), projection_grads, weight_grad_out)


LANES = 128
F32 = jnp.float32
BF16 = jnp.bfloat16


def dot(left, right, left_dim, right_dim):
    return lax.dot_general(
        left, right, (((left_dim,), (right_dim,)), ((), ())), preferred_element_type=F32
    )


def norm_lanes(values):
    center = values - jnp.mean(values, axis=1, keepdims=True)
    inverse = lax.rsqrt(jnp.mean(center * center, axis=1, keepdims=True) + EPSILON)
    return center * inverse, inverse


def norm_lanes_back(grad, normed, inverse, gain):
    scaled = grad * gain
    centered = scaled - jnp.mean(scaled, axis=1, keepdims=True)
    return (centered - normed * jnp.mean(scaled * normed, axis=1, keepdims=True)) * inverse


def fused_kernel(
    n,
    rows,
    residues,
    pair_hbm,
    chain_hbm,
    mask_hbm,
    table_hbm,
    gain_hbm,
    shift_hbm,
    proj_hbm,
    weight_hbm,
    cot_hbm,
    grad_out,
    proj_out,
    weight_out,
    stream,
    mask,
    normed_in,
    inverse_in,
    normed_out,
    inverse_out,
    activated,
    pre,
    mixture,
    update,
    up,
    mix_grad,
    update_grad,
    pre_grad,
    factors,
    stage16,
    stage8,
    rows16,
    rows8,
    wide_send,
    wide_recv,
    thin_send,
    thin_recv,
    early_send,
    late_send,
    early_recv,
    late_recv,
    early_share,
    late_share,
    early_all,
    late_all,
    total,
    send_sem,
    recv_sem,
    load_sem,
    pair_ref,
    chain_ref,
    mask_ref,
    table_ref,
    gain_ref,
    shift_ref,
    proj_ref,
    weight_ref,
    cot_ref,
):
    channels = LANES
    slices = channels // n
    padded = factors.shape[-1]
    pairs = rows * residues
    double = 2 * slices
    me = lax.axis_index("dap")
    barrier = pltpu.get_barrier_semaphore()

    def each_peer(body):
        def step(index, carry):
            reach = n // 2 + (1 - 2 * lax.rem(index, 2)) * ((index + 1) // 2)
            body(lax.rem(me + reach, n))
            return carry

        lax.fori_loop(0, n - 1, step, 0)

    def greet(peer):
        pl.semaphore_signal(
            barrier, inc=1, device_id={"dap": peer}, device_id_type=pl.DeviceIdType.MESH
        )

    each_peer(greet)
    loads = [
        pltpu.make_async_copy(source, target, load_sem.at[place])
        for place, (source, target) in enumerate(
            (
                (chain_hbm, chain_ref),
                (mask_hbm, mask_ref),
                (table_hbm, table_ref),
                (pair_hbm, pair_ref),
                (gain_hbm, gain_ref),
                (shift_hbm, shift_ref),
                (proj_hbm, proj_ref),
                (weight_hbm, weight_ref),
                (cot_hbm, cot_ref),
            )
        )
    ]
    for load in loads:
        load.start()

    def copy(phase, source, target, peer, owner):
        return pltpu.make_async_remote_copy(
            src_ref=source,
            dst_ref=target.at[owner],
            send_sem=send_sem.at[phase, peer],
            recv_sem=recv_sem.at[phase, owner],
            device_id={"dap": peer},
            device_id_type=pl.DeviceIdType.MESH,
        )

    def send_all(phase, source_of, target):
        target[me] = source_of(me)[...]
        each_peer(lambda peer: copy(phase, source_of(peer), target, peer, me).start())

    def take_all(phase, source_of, target):
        each_peer(lambda peer: copy(phase, source_of(peer), target, peer, peer).wait_recv())

    def end_all(phase, source_of, target):
        each_peer(lambda peer: copy(phase, source_of(peer), target, peer, me).wait_send())

    def span(row):
        return pl.ds(row * residues, residues)

    upper = (rows + 1) // 2
    halves = ((0, upper), (upper, rows))
    wide_lanes = wide_send.shape[-1]
    thin_lanes = thin_send.shape[-1]

    def to_columns(values, lanes):
        filler = jnp.zeros((lanes - values.shape[0], channels), F32)
        return jnp.concatenate([values, filler], axis=0).T.reshape(n, slices, lanes)

    def to_rows(blocks, count):
        return blocks.reshape(channels, blocks.shape[-1]).T[:count]

    def pack(tiles, lanes):
        filler = jnp.zeros((tiles[0].shape[0], lanes - len(tiles) * residues), F32)
        return jnp.concatenate(tiles + [filler], axis=1)

    def wide(number):
        return lambda peer: wide_send.at[number, peer]

    def thin(number):
        return lambda peer: thin_send.at[number, peer]

    def shares(sums, share):
        return lambda peer: sums.at[pl.ds(pl.multiple_of(peer * share, 16), share)]

    exchanges = {
        0: (wide(0), wide_recv.at[0]),
        1: (thin(0), thin_recv.at[0]),
        2: (wide(1), wide_recv.at[1]),
        3: (thin(1), thin_recv.at[1]),
        4: (thin(2), thin_recv.at[2]),
        5: (wide(2), wide_recv.at[2]),
        6: (thin(3), thin_recv.at[3]),
        7: (wide(3), wide_recv.at[3]),
        8: (shares(early_send, early_recv.shape[1]), early_recv),
        9: (lambda peer: early_share, early_all),
        10: (shares(late_send, late_recv.shape[1]), late_recv),
        11: (lambda peer: late_share, late_all),
    }

    stage16[...] = jnp.zeros_like(stage16)
    stage8[...] = jnp.zeros_like(stage8)

    for load in loads:
        load.wait()
    chain = chain_ref[...]
    place = lax.broadcasted_iota(jnp.int32, chain.shape, 1)
    for row in range(rows):
        own = jnp.sum(jnp.where(place == me * rows + row, chain, 0), axis=1, keepdims=True)
        same = jnp.where(chain == own, 1.0, 0.0).astype(F32)
        filler = jnp.zeros((1, padded - residues), F32)
        seen = mask_ref[pl.ds(row, 1), :].astype(F32)
        if padded > residues:
            same = jnp.concatenate([same, filler], axis=1)
            seen = jnp.concatenate([seen, filler], axis=1)
        same = jnp.broadcast_to(same, (channels, padded)).T[:residues]
        mask[span(row), :] = jnp.broadcast_to(seen, (channels, padded)).T[:residues]
        stream[0, span(row), :] = pair_ref[row].astype(F32) + jnp.where(
            same > 0.5, table_ref[1:2, :], table_ref[0:1, :]
        )

    def send_factors(number):
        gain, shift = gain_ref[number, 0:1, :], shift_ref[number, 0:1, :]
        for row in range(rows):
            normed, inverse = norm_lanes(stream[number, span(row), :])
            normed_in[number, span(row), :] = normed
            inverse_in[number, span(row), :] = jnp.broadcast_to(inverse, normed.shape)
            activated[number, span(row), :] = (normed * gain + shift).astype(BF16)
        for part in range(5):
            pre[number, part] = dot(activated[number], proj_ref[number, part], 1, 0)
        left = mask[...] * jax.nn.sigmoid(pre[number, 1]) * pre[number, 0]
        right = mask[...] * jax.nn.sigmoid(pre[number, 3]) * pre[number, 2]
        both = jnp.concatenate(
            [to_columns(left, wide_lanes), to_columns(right, wide_lanes)], axis=1
        )
        wide_send[number] = both.astype(BF16)
        if number == 0:
            pl.semaphore_wait(barrier, n - 1)
        send_all(2 * number, *exchanges[2 * number])

    def send_product(number):
        take_all(2 * number, *exchanges[2 * number])
        for owner in range(n):
            block = wide_recv[number, owner].astype(F32)
            for row in range(rows):
                stage16[pl.ds((owner * rows + row) * double, double), :residues] = block[
                    :, row * residues : (row + 1) * residues
                ]
        for channel in range(slices):
            left = stage16[pl.ds(channel, padded, stride=double), :].astype(BF16)
            right = stage16[pl.ds(slices + channel, padded, stride=double), :].astype(BF16)
            factors[number, 0, channel] = left
            factors[number, 1, channel] = right
            stage8[pl.ds(channel, padded, stride=slices), :] = dot(
                left, right, 1 - number, 1 - number
            )
        for owner in range(n):
            packed = [
                pack(
                    [
                        stage8[pl.ds((owner * rows + row) * slices, slices), :residues]
                        for row in range(*half)
                    ],
                    thin_lanes,
                )
                for half in halves
            ]
            thin_send[number, owner] = jnp.concatenate(packed, axis=0).astype(BF16)
        send_all(2 * number + 1, *exchanges[2 * number + 1])

    def take_product(number):
        take_all(2 * number + 1, *exchanges[2 * number + 1])
        gain, shift = gain_ref[number, 1:2, :], shift_ref[number, 1:2, :]
        rows8[...] = thin_recv[number].astype(F32)
        for place, (first, last) in enumerate(halves):
            count = (last - first) * residues
            product = to_rows(rows8[:, pl.ds(place * slices, slices), :], count)
            normed, inverse = norm_lanes(product)
            where = pl.ds(first * residues, count)
            normed_out[number, where, :] = normed
            inverse_out[number, where, :] = jnp.broadcast_to(inverse, normed.shape)
            mixture[number, where, :] = (normed * gain + shift).astype(BF16)

    def take_update(number):
        update[number] = dot(mixture[number], weight_ref[number], 1, 0)

    def mixture_back(number):
        for row in range(rows):
            gate = jax.nn.sigmoid(pre[number, 4, span(row)])
            update_grad[number, span(row), :] = (up[number, span(row)] * gate).astype(BF16)
        mix_grad[...] = dot(update_grad[number], weight_ref[number], 1, 1)

    def send_product_grad(number):
        gain = gain_ref[number, 1:2, :]
        packed = []
        for first, last in halves:
            where = pl.ds(first * residues, (last - first) * residues)
            grad = norm_lanes_back(
                mix_grad[where, :],
                normed_out[number, where, :],
                inverse_out[number, where, :],
                gain,
            )
            packed.append(to_columns(grad, thin_lanes))
        thin_send[3 - number] = jnp.concatenate(packed, axis=1).astype(BF16)
        send_all(6 - 2 * number, *exchanges[6 - 2 * number])

    def gate_back(number):
        for row in range(rows):
            gate = jax.nn.sigmoid(pre[number, 4, span(row)])
            pre_grad[number, 4, span(row), :] = (
                up[number, span(row)] * update[number, span(row)] * gate * (1.0 - gate)
            ).astype(BF16)

    def weight_sum(number, part):
        if part == 5:
            grad = dot(mixture[number], update_grad[number], 0, 0)
        else:
            grad = dot(activated[number], pre_grad[number, part], 0, 0)
        grad = (grad * (1.0 / residues)).astype(BF16)
        if number == 0 and part < 4:
            late_send[pl.ds(part * channels, channels), :] = grad
        else:
            slot = part if number == 1 else part + 2
            early_send[pl.ds(slot * channels, channels), :] = grad

    def send_factor_grads(number):
        phase = 6 - 2 * number
        take_all(phase, *exchanges[phase])
        for owner in range(n):
            block = thin_recv[3 - number, owner].astype(F32)
            for place, (first, last) in enumerate(halves):
                for row in range(first, last):
                    lane = (row - first) * residues
                    stage8[pl.ds((owner * rows + row) * slices, slices), :residues] = block[
                        place * slices : (place + 1) * slices, lane : lane + residues
                    ]
        for channel in range(slices):
            grad = stage8[pl.ds(channel, padded, stride=slices), :].astype(BF16)
            left, right = factors[number, 0, channel], factors[number, 1, channel]
            if number == 0:
                left_grad = dot(grad, right, 1, 0)
                right_grad = dot(grad, left, 0, 0)
            else:
                left_grad = dot(right, grad, 1, 1)
                right_grad = dot(left, grad, 1, 0)
            stage16[pl.ds(channel, padded, stride=double), :] = left_grad
            stage16[pl.ds(slices + channel, padded, stride=double), :] = right_grad
        for owner in range(n):
            wide_send[3 - number, owner] = pack(
                [
                    stage16[pl.ds((owner * rows + row) * double, double), :residues]
                    for row in range(rows)
                ],
                wide_lanes,
            ).astype(BF16)
        send_all(phase + 1, *exchanges[phase + 1])

    def take_factor_grads(number):
        phase = 7 - 2 * number
        take_all(phase, *exchanges[phase])
        rows16[...] = wide_recv[3 - number].astype(F32)
        for side in range(2):
            grad = to_rows(rows16[:, pl.ds(side * slices, slices), :], pairs)
            gate = jax.nn.sigmoid(pre[number, 2 * side + 1])
            opened = mask[...] * grad * gate
            pre_grad[number, 2 * side] = opened.astype(BF16)
            pre_grad[number, 2 * side + 1] = (
                opened * pre[number, 2 * side] * (1.0 - gate)
            ).astype(BF16)

    def stream_back(number):
        inner = dot(pre_grad[number, 0], proj_ref[number, 0], 1, 1)
        for part in range(1, 5):
            inner = inner + dot(pre_grad[number, part], proj_ref[number, part], 1, 1)
        mix_grad[...] = inner
        gain = gain_ref[number, 0:1, :]
        for row in range(rows):
            grad = up[number, span(row)] + norm_lanes_back(
                mix_grad[span(row), :],
                normed_in[number, span(row), :],
                inverse_in[number, span(row), :],
                gain,
            )
            if number == 1:
                up[0, span(row), :] = grad
            else:
                grad_out[row] = grad.astype(BF16)

    def send_total(phase, parts, share):
        take_all(phase, *exchanges[phase])
        result = parts[0].astype(F32)
        for owner in range(1, n):
            result = result + parts[owner].astype(F32)
        share[...] = result.astype(BF16)
        send_all(phase + 1, *exchanges[phase + 1])

    def take_total(phase, blocks):
        take_all(phase, *exchanges[phase])
        share = blocks.shape[1]
        for owner in range(n):
            total[pl.ds(owner * share, share), :] = blocks[owner].astype(F32)

    def part_of(slot):
        return total[pl.ds(slot * channels, channels), :]

    send_factors(0)
    up[1] = cot_ref[...].reshape(pairs, channels).astype(F32)
    send_product(0)
    take_product(0)
    take_update(0)
    for row in range(rows):
        gate = jax.nn.sigmoid(pre[0, 4, span(row)])
        stream[1, span(row), :] = (
            (stream[0, span(row), :] + gate * update[0, span(row)]).astype(BF16).astype(F32)
        )
    send_factors(1)
    mixture_back(1)
    send_product(1)
    take_product(1)
    send_product_grad(1)
    take_update(1)
    gate_back(1)
    send_factor_grads(1)
    weight_sum(1, 4)
    weight_sum(1, 5)
    take_factor_grads(1)
    stream_back(1)
    mixture_back(0)
    send_product_grad(0)
    gate_back(0)
    for part in range(4):
        weight_sum(1, part)
    weight_sum(0, 4)
    weight_sum(0, 5)
    send_all(8, *exchanges[8])
    send_factor_grads(0)
    send_total(8, early_recv, early_share)
    take_factor_grads(0)
    for part in range(4):
        weight_sum(0, part)
    send_all(10, *exchanges[10])
    stream_back(0)
    take_total(9, early_all)
    for part in range(5):
        proj_out[1, part] = part_of(part)
    weight_out[1] = part_of(5)
    proj_out[0, 4] = part_of(6)
    weight_out[0] = part_of(7)
    send_total(10, late_recv, late_share)
    take_total(11, late_all)
    for part in range(4):
        proj_out[0, part] = part_of(part)
    for phase in range(12):
        end_all(phase, *exchanges[phase])


def fused(
    pair_state,
    chain_index,
    pair_mask,
    chain_table,
    norm_gain,
    norm_shift,
    projections,
    output_weight,
    cotangent,
):
    rows, residues, channels = pair_state.shape
    n = lax.axis_size("dap")
    slices = channels // n
    padded = -(-residues // LANES) * LANES
    pairs = rows * residues
    double = 2 * slices
    wide = -(-pairs // LANES) * LANES
    thin = -(-((rows + 1) // 2) * residues // LANES) * LANES
    early, late = 8 * channels // n, 4 * channels // n
    vmem = pl.BlockSpec(memory_space=pltpu.VMEM)
    return pl.pallas_call(
        functools.partial(fused_kernel, n, rows, residues),
        out_shape=(
            jax.ShapeDtypeStruct((rows, residues, channels), BF16),
            jax.ShapeDtypeStruct((2, 5, channels, channels), F32),
            jax.ShapeDtypeStruct((2, channels, channels), F32),
        ),
        in_specs=[pl.BlockSpec(memory_space=pltpu.HBM)] * 9,
        out_specs=(vmem,) * 3,
        scratch_shapes=[
            pltpu.VMEM((2, pairs, channels), F32),
            pltpu.VMEM((pairs, channels), F32),
            pltpu.VMEM((2, pairs, channels), F32),
            pltpu.VMEM((2, pairs, channels), F32),
            pltpu.VMEM((2, pairs, channels), F32),
            pltpu.VMEM((2, pairs, channels), F32),
            pltpu.VMEM((2, pairs, channels), BF16),
            pltpu.VMEM((2, 5, pairs, channels), F32),
            pltpu.VMEM((2, pairs, channels), BF16),
            pltpu.VMEM((2, pairs, channels), F32),
            pltpu.VMEM((2, pairs, channels), F32),
            pltpu.VMEM((pairs, channels), F32),
            pltpu.VMEM((2, pairs, channels), BF16),
            pltpu.VMEM((2, 5, pairs, channels), BF16),
            pltpu.VMEM((2, 2, slices, padded, padded), BF16),
            pltpu.VMEM((padded * 2 * slices, padded), F32),
            pltpu.VMEM((padded * slices, padded), F32),
            pltpu.VMEM((n, double, wide), F32),
            pltpu.VMEM((n, double, thin), F32),
            pltpu.VMEM((4, n, double, wide), BF16),
            pltpu.VMEM((4, n, double, wide), BF16),
            pltpu.VMEM((4, n, double, thin), BF16),
            pltpu.VMEM((4, n, double, thin), BF16),
            pltpu.VMEM((8 * channels, channels), BF16),
            pltpu.VMEM((4 * channels, channels), BF16),
            pltpu.VMEM((n, early, channels), BF16),
            pltpu.VMEM((n, late, channels), BF16),
            pltpu.VMEM((early, channels), BF16),
            pltpu.VMEM((late, channels), BF16),
            pltpu.VMEM((n, early, channels), BF16),
            pltpu.VMEM((n, late, channels), BF16),
            pltpu.VMEM((8 * channels, channels), F32),
            pltpu.SemaphoreType.DMA((12, n)),
            pltpu.SemaphoreType.DMA((12, n)),
            pltpu.SemaphoreType.DMA((9,)),
            pltpu.VMEM((rows, residues, channels), BF16),
            pltpu.VMEM((1, residues), jnp.int32),
            pltpu.VMEM((rows, residues), jnp.int32),
            pltpu.VMEM((2, channels), F32),
            pltpu.VMEM((2, 2, channels), F32),
            pltpu.VMEM((2, 2, channels), F32),
            pltpu.VMEM((2, 5, channels, channels), BF16),
            pltpu.VMEM((2, channels, channels), BF16),
            pltpu.VMEM((rows, residues, channels), BF16),
        ],
        compiler_params=pltpu.CompilerParams(
            collective_id=0, has_side_effects=True, vmem_limit_bytes=40 * 2**20
        ),
    )(
        pair_state,
        chain_index.reshape(1, residues),
        pair_mask,
        chain_table,
        norm_gain,
        norm_shift,
        projections,
        output_weight,
        cotangent,
    )


def fits(rows, residues, channels, n):
    padded = -(-residues // LANES) * LANES
    return (
        channels == LANES
        and channels % n == 0
        and (channels // n) % 8 == 0
        and (4 * channels // n) % 16 == 0
        and n % 2 == 0
        and residues % 16 == 0
        and padded <= 2 * LANES
    )


def shards(*arguments):
    rows, residues, channels = arguments[0].shape
    n = lax.axis_size("dap")
    if fits(rows, residues, channels, n):
        return fused(*arguments)
    return sharded_ops(*arguments)


def solution(mesh):
    return jax.shard_map(
        shards,
        mesh=mesh,
        in_specs=(
            P(("groups", "dap"), None, None),
            P("groups"),
            P(("groups", "dap"), None),
            P(),
            P(),
            P(),
            P(),
            P(),
            P(("groups", "dap"), None, None),
        ),
        out_specs=(
            P(("groups", "dap"), None, None),
            P("groups", None, None, None),
            P("groups", None, None),
        ),
        check_vma=False,
    )
```

```python
import functools

import jax
import jax.numpy as jnp
from jax import lax
from jax.experimental import pallas as pl
from jax.experimental.pallas import tpu as pltpu
from jax.sharding import PartitionSpec as P

EPSILON = 1e-05


def normalize(values, norm_gain, norm_shift, reduce_axis):
    center = values - jnp.mean(values, axis=reduce_axis, keepdims=True)
    inverse = lax.rsqrt(jnp.mean(center * center, axis=reduce_axis, keepdims=True) + EPSILON)
    normed = center * inverse
    return (normed, inverse, normed * norm_gain + norm_shift)


def normalize_back(grad_output, normed, inverse, norm_gain, reduce_axis):
    scaled = grad_output * norm_gain
    centered = scaled - jnp.mean(scaled, axis=reduce_axis, keepdims=True)
    return (
        centered - normed * jnp.mean(scaled * normed, axis=reduce_axis, keepdims=True)
    ) * inverse


def multiply(left_cols, right_cols, incoming):
    if incoming:
        return jnp.einsum(
            "xcki,xckj->xcij", left_cols, right_cols, preferred_element_type=jnp.float32
        )
    return jnp.einsum("xcik,xcjk->xcij", left_cols, right_cols, preferred_element_type=jnp.float32)


def factor_grads(grad_cols, left_cols, right_cols, incoming):
    if incoming:
        left_grad = jnp.einsum(
            "xcij,xckj->xcki", grad_cols, right_cols, preferred_element_type=jnp.float32
        )
        right_grad = jnp.einsum(
            "xcij,xcki->xckj", grad_cols, left_cols, preferred_element_type=jnp.float32
        )
    else:
        left_grad = jnp.einsum(
            "xcij,xcjk->xcik", grad_cols, right_cols, preferred_element_type=jnp.float32
        )
        right_grad = jnp.einsum(
            "xcij,xcik->xcjk", grad_cols, left_cols, preferred_element_type=jnp.float32
        )
    return (left_grad.astype(jnp.bfloat16), right_grad.astype(jnp.bfloat16))


def block_forward(stream, masked, norm_gains, norm_shifts, weights, out_weight, incoming):
    rows, residues, channels = stream.shape
    devices = lax.axis_size("dap")
    slices = channels // devices
    normed_in, inverse_in, scaled_in = normalize(stream, norm_gains[0], norm_shifts[0], 2)
    activated = scaled_in.astype(jnp.bfloat16)
    factor_pre = jnp.einsum(
        "rnd,pdc->pcrn", activated, weights[:4], preferred_element_type=jnp.float32
    )
    gate_pre = jnp.einsum("rnd,dc->rnc", activated, weights[4], preferred_element_type=jnp.float32)
    gate_left = jax.nn.sigmoid(factor_pre[1])
    gate_right = jax.nn.sigmoid(factor_pre[3])
    left_factor = (masked * gate_left * factor_pre[0]).astype(jnp.bfloat16)
    right_factor = (masked * gate_right * factor_pre[2]).astype(jnp.bfloat16)
    left_blocks = left_factor.reshape(devices, slices, rows, residues)
    right_blocks = right_factor.reshape(devices, slices, rows, residues)
    left_cols, right_cols = (
        lax.all_to_all(left_blocks, "dap", split_axis=0, concat_axis=2, tiled=True),
        lax.all_to_all(right_blocks, "dap", split_axis=0, concat_axis=2, tiled=True),
    )
    product = multiply(left_cols, right_cols, incoming).astype(jnp.bfloat16)
    returned = lax.all_to_all(product, "dap", split_axis=2, concat_axis=0, tiled=True)
    product_rows = returned.reshape(channels, rows, residues)
    normed_out, inverse_out, scaled_out = normalize(
        product_rows.astype(jnp.float32),
        norm_gains[1][:, None, None],
        norm_shifts[1][:, None, None],
        0,
    )
    mixture = scaled_out.astype(jnp.bfloat16)
    update = jnp.einsum("crn,cd->rnd", mixture, out_weight, preferred_element_type=jnp.float32)
    out_gate = jax.nn.sigmoid(gate_pre)
    following = (stream + out_gate * update).astype(jnp.bfloat16)
    stored = (
        activated,
        factor_pre,
        left_cols,
        right_cols,
        normed_out,
        inverse_out,
        mixture,
        update,
        out_gate,
        normed_in,
        inverse_in,
    )
    return (following, stored)


def block_backward(upstream, stored, masked, norm_gains, weights, out_weight, incoming):
    (
        activated,
        factor_pre,
        left_cols,
        right_cols,
        normed_out,
        inverse_out,
        mixture,
        update,
        out_gate,
        normed_in,
        inverse_in,
    ) = stored
    rows, residues, channels = upstream.shape
    devices = lax.axis_size("dap")
    slices = channels // devices
    update_grad = (upstream * out_gate).astype(jnp.bfloat16)
    gate_grad = (upstream * update * out_gate * (1.0 - out_gate)).astype(jnp.bfloat16)
    out_weight_grad = jnp.einsum(
        "crn,rnd->cd", mixture, update_grad, preferred_element_type=jnp.float32
    )
    mixture_grad = jnp.einsum(
        "rnd,cd->crn", update_grad, out_weight, preferred_element_type=jnp.float32
    )
    product_grad = normalize_back(
        mixture_grad, normed_out, inverse_out, norm_gains[1][:, None, None], 0
    ).astype(jnp.bfloat16)
    grad_blocks = product_grad.reshape(devices, slices, rows, residues)
    grad_cols = lax.all_to_all(grad_blocks, "dap", split_axis=0, concat_axis=2, tiled=True)
    left_grad, right_grad = factor_grads(grad_cols, left_cols, right_cols, incoming)
    left_back, right_back = (
        lax.all_to_all(left_grad, "dap", split_axis=2, concat_axis=0, tiled=True),
        lax.all_to_all(right_grad, "dap", split_axis=2, concat_axis=0, tiled=True),
    )
    left_rows = left_back.reshape(channels, rows, residues).astype(jnp.float32)
    right_rows = right_back.reshape(channels, rows, residues).astype(jnp.float32)
    gate_left = jax.nn.sigmoid(factor_pre[1])
    gate_right = jax.nn.sigmoid(factor_pre[3])
    factor_grad = jnp.stack(
        [
            left_rows * masked * gate_left,
            left_rows * masked * factor_pre[0] * gate_left * (1.0 - gate_left),
            right_rows * masked * gate_right,
            right_rows * masked * factor_pre[2] * gate_right * (1.0 - gate_right),
        ]
    ).astype(jnp.bfloat16)
    factor_weight_grads = jnp.einsum(
        "rnd,pcrn->pdc", activated, factor_grad, preferred_element_type=jnp.float32
    )
    gate_weight_grad = jnp.einsum(
        "rnd,rnc->dc", activated, gate_grad, preferred_element_type=jnp.float32
    )
    weight_grads = jnp.concatenate([factor_weight_grads, gate_weight_grad[None]], 0)
    input_grad = jnp.einsum(
        "pcrn,pdc->rnd", factor_grad, weights[:4], preferred_element_type=jnp.float32
    )
    input_grad = input_grad + jnp.einsum(
        "rnc,dc->rnd", gate_grad, weights[4], preferred_element_type=jnp.float32
    )
    stream_grad = upstream + normalize_back(input_grad, normed_in, inverse_in, norm_gains[0], 2)
    return (stream_grad, weight_grads, out_weight_grad)


def reduce_block(weight_grads, out_weight_grad):
    return lax.psum((weight_grads, out_weight_grad), "dap")


def sharded_ops(
    pair_state,
    chain_index,
    pair_mask,
    chain_table,
    norm_gain,
    norm_shift,
    projections,
    output_weight,
    cotangent,
):
    rows, residues, channels = pair_state.shape
    first_row = lax.axis_index("dap") * rows
    own_chain = lax.dynamic_slice_in_dim(chain_index, first_row, rows, 0)
    same_chain = own_chain[:, None] == chain_index[None, :]
    stream = pair_state.astype(jnp.float32) + jnp.where(
        same_chain[:, :, None], chain_table[1], chain_table[0]
    )
    masked = pair_mask.astype(jnp.float32)[None]
    following, stored_first = block_forward(
        stream, masked, norm_gain[0], norm_shift[0], projections[0], output_weight[0], False
    )
    ignored, stored_second = block_forward(
        following.astype(jnp.float32),
        masked,
        norm_gain[1],
        norm_shift[1],
        projections[1],
        output_weight[1],
        True,
    )
    grad_mid, proj_second, out_second = block_backward(
        cotangent.astype(jnp.float32),
        stored_second,
        masked,
        norm_gain[1],
        projections[1],
        output_weight[1],
        True,
    )
    proj_second, out_second = reduce_block(proj_second, out_second)
    grad_first, proj_first, out_first = block_backward(
        grad_mid, stored_first, masked, norm_gain[0], projections[0], output_weight[0], False
    )
    proj_first, out_first = reduce_block(proj_first, out_first)
    scale_rows = 1.0 / residues
    projection_grads = jnp.stack([proj_first, proj_second]) * scale_rows
    weight_grad_out = jnp.stack([out_first, out_second]) * scale_rows
    return (grad_first.astype(jnp.bfloat16), projection_grads, weight_grad_out)


LANES = 128
F32 = jnp.float32
BF16 = jnp.bfloat16


def dot(left, right, left_dim, right_dim):
    return lax.dot_general(
        left, right, (((left_dim,), (right_dim,)), ((), ())), preferred_element_type=F32
    )


def norm_lanes(values):
    center = values - jnp.mean(values, axis=1, keepdims=True)
    inverse = lax.rsqrt(jnp.mean(center * center, axis=1, keepdims=True) + EPSILON)
    return center * inverse, inverse


def norm_lanes_back(grad, normed, inverse, gain):
    scaled = grad * gain
    centered = scaled - jnp.mean(scaled, axis=1, keepdims=True)
    return (centered - normed * jnp.mean(scaled * normed, axis=1, keepdims=True)) * inverse


def fused_kernel(
    n,
    rows,
    residues,
    pair_hbm,
    chain_hbm,
    mask_hbm,
    table_hbm,
    gain_hbm,
    shift_hbm,
    proj_hbm,
    weight_hbm,
    cot_hbm,
    grad_out,
    proj_out,
    weight_out,
    stream,
    mask,
    normed_in,
    inverse_in,
    normed_out,
    inverse_out,
    activated,
    pre,
    mixture,
    update,
    up,
    mix_grad,
    update_grad,
    pre_grad,
    factors,
    stage16,
    stage8,
    rows16,
    rows8,
    wide_send,
    wide_recv,
    thin_send,
    thin_recv,
    early_send,
    late_send,
    early_recv,
    late_recv,
    early_share,
    late_share,
    early_all,
    late_all,
    total,
    send_sem,
    recv_sem,
    load_sem,
    pair_ref,
    chain_ref,
    mask_ref,
    table_ref,
    gain_ref,
    shift_ref,
    proj_ref,
    weight_ref,
    cot_ref,
):
    channels = LANES
    slices = channels // n
    padded = factors.shape[-1]
    pairs = rows * residues
    double = 2 * slices
    me = lax.axis_index("dap")
    barrier = pltpu.get_barrier_semaphore()

    def each_peer(body, unrolled=False):
        def step(index, carry):
            body(lax.rem(me + index, n))
            return carry

        lax.fori_loop(1, n, step, 0, unroll=n - 1 if unrolled else 1)

    def greet(peer):
        pl.semaphore_signal(
            barrier, inc=1, device_id={"dap": peer}, device_id_type=pl.DeviceIdType.MESH
        )

    each_peer(greet)
    loads = [
        pltpu.make_async_copy(source, target, load_sem.at[place])
        for place, (source, target) in enumerate(
            (
                (chain_hbm, chain_ref),
                (mask_hbm, mask_ref),
                (table_hbm, table_ref),
                (pair_hbm, pair_ref),
                (gain_hbm, gain_ref),
                (shift_hbm, shift_ref),
                (proj_hbm, proj_ref),
                (weight_hbm, weight_ref),
                (cot_hbm, cot_ref),
            )
        )
    ]
    for load in loads:
        load.start()

    def copy(phase, source, target, peer, owner):
        return pltpu.make_async_remote_copy(
            src_ref=source,
            dst_ref=target.at[owner],
            send_sem=send_sem.at[phase, peer],
            recv_sem=recv_sem.at[phase, owner],
            device_id={"dap": peer},
            device_id_type=pl.DeviceIdType.MESH,
        )

    def send_all(phase, source_of, target):
        each_peer(lambda peer: copy(phase, source_of(peer), target, peer, me).start(), True)
        target[me] = source_of(me)[...]

    def take_all(phase, source_of, target):
        each_peer(lambda peer: copy(phase, source_of(peer), target, peer, peer).wait_recv())

    def end_all(phase, source_of, target):
        each_peer(lambda peer: copy(phase, source_of(peer), target, peer, me).wait_send())

    def span(row):
        return pl.ds(row * residues, residues)

    upper = (rows + 1) // 2
    halves = ((0, upper), (upper, rows))
    wide_lanes = wide_send.shape[-1]
    thin_lanes = thin_send.shape[-1]

    def to_columns(values, lanes):
        filler = jnp.zeros((lanes - values.shape[0], channels), F32)
        return jnp.concatenate([values, filler], axis=0).T.reshape(n, slices, lanes)

    def to_rows(blocks, count):
        return blocks.reshape(channels, blocks.shape[-1]).T[:count]

    def pack(tiles, lanes):
        filler = jnp.zeros((tiles[0].shape[0], lanes - len(tiles) * residues), F32)
        return jnp.concatenate(tiles + [filler], axis=1)

    def wide(number):
        return lambda peer: wide_send.at[number, peer]

    def thin(number):
        return lambda peer: thin_send.at[number, peer]

    def shares(sums, share):
        return lambda peer: sums.at[pl.ds(pl.multiple_of(peer * share, 16), share)]

    exchanges = {
        0: (wide(0), wide_recv.at[0]),
        1: (thin(0), thin_recv.at[0]),
        2: (wide(1), wide_recv.at[1]),
        3: (thin(1), thin_recv.at[1]),
        4: (thin(2), thin_recv.at[2]),
        5: (wide(2), wide_recv.at[2]),
        6: (thin(3), thin_recv.at[3]),
        7: (wide(3), wide_recv.at[3]),
        8: (shares(early_send, early_recv.shape[1]), early_recv),
        9: (lambda peer: early_share, early_all),
        10: (shares(late_send, late_recv.shape[1]), late_recv),
        11: (lambda peer: late_share, late_all),
    }

    stage16[...] = jnp.zeros_like(stage16)
    stage8[...] = jnp.zeros_like(stage8)

    for load in loads:
        load.wait()
    chain = chain_ref[...]
    place = lax.broadcasted_iota(jnp.int32, chain.shape, 1)
    for row in range(rows):
        own = jnp.sum(jnp.where(place == me * rows + row, chain, 0), axis=1, keepdims=True)
        same = jnp.where(chain == own, 1.0, 0.0).astype(F32)
        filler = jnp.zeros((1, padded - residues), F32)
        seen = mask_ref[pl.ds(row, 1), :].astype(F32)
        if padded > residues:
            same = jnp.concatenate([same, filler], axis=1)
            seen = jnp.concatenate([seen, filler], axis=1)
        same = jnp.broadcast_to(same, (channels, padded)).T[:residues]
        mask[span(row), :] = jnp.broadcast_to(seen, (channels, padded)).T[:residues]
        stream[0, span(row), :] = pair_ref[row].astype(F32) + jnp.where(
            same > 0.5, table_ref[1:2, :], table_ref[0:1, :]
        )

    def send_factors(number):
        gain, shift = gain_ref[number, 0:1, :], shift_ref[number, 0:1, :]
        for row in range(rows):
            normed, inverse = norm_lanes(stream[number, span(row), :])
            normed_in[number, span(row), :] = normed
            inverse_in[number, span(row), :] = jnp.broadcast_to(inverse, normed.shape)
            activated[number, span(row), :] = (normed * gain + shift).astype(BF16)
        for part in range(5):
            pre[number, part] = dot(activated[number], proj_ref[number, part], 1, 0)
        left = mask[...] * jax.nn.sigmoid(pre[number, 1]) * pre[number, 0]
        right = mask[...] * jax.nn.sigmoid(pre[number, 3]) * pre[number, 2]
        both = jnp.concatenate(
            [to_columns(left, wide_lanes), to_columns(right, wide_lanes)], axis=1
        )
        wide_send[number] = both.astype(BF16)
        if number == 0:
            pl.semaphore_wait(barrier, n - 1)
        send_all(2 * number, *exchanges[2 * number])

    def send_product(number):
        take_all(2 * number, *exchanges[2 * number])
        for owner in range(n):
            block = wide_recv[number, owner].astype(F32)
            for row in range(rows):
                stage16[pl.ds((owner * rows + row) * double, double), :residues] = block[
                    :, row * residues : (row + 1) * residues
                ]
        for channel in range(slices):
            left = stage16[pl.ds(channel, padded, stride=double), :].astype(BF16)
            right = stage16[pl.ds(slices + channel, padded, stride=double), :].astype(BF16)
            factors[number, 0, channel] = left
            factors[number, 1, channel] = right
            stage8[pl.ds(channel, padded, stride=slices), :] = dot(
                left, right, 1 - number, 1 - number
            )
        for owner in range(n):
            packed = [
                pack(
                    [
                        stage8[pl.ds((owner * rows + row) * slices, slices), :residues]
                        for row in range(*half)
                    ],
                    thin_lanes,
                )
                for half in halves
            ]
            thin_send[number, owner] = jnp.concatenate(packed, axis=0).astype(BF16)
        send_all(2 * number + 1, *exchanges[2 * number + 1])

    def take_product(number):
        take_all(2 * number + 1, *exchanges[2 * number + 1])
        gain, shift = gain_ref[number, 1:2, :], shift_ref[number, 1:2, :]
        rows8[...] = thin_recv[number].astype(F32)
        for place, (first, last) in enumerate(halves):
            count = (last - first) * residues
            product = to_rows(rows8[:, pl.ds(place * slices, slices), :], count)
            normed, inverse = norm_lanes(product)
            where = pl.ds(first * residues, count)
            normed_out[number, where, :] = normed
            inverse_out[number, where, :] = jnp.broadcast_to(inverse, normed.shape)
            mixture[number, where, :] = (normed * gain + shift).astype(BF16)

    def take_update(number):
        update[number] = dot(mixture[number], weight_ref[number], 1, 0)

    def mixture_back(number):
        for row in range(rows):
            gate = jax.nn.sigmoid(pre[number, 4, span(row)])
            update_grad[number, span(row), :] = (up[number, span(row)] * gate).astype(BF16)
        mix_grad[...] = dot(update_grad[number], weight_ref[number], 1, 1)

    def send_product_grad(number):
        gain = gain_ref[number, 1:2, :]
        packed = []
        for first, last in halves:
            where = pl.ds(first * residues, (last - first) * residues)
            grad = norm_lanes_back(
                mix_grad[where, :],
                normed_out[number, where, :],
                inverse_out[number, where, :],
                gain,
            )
            packed.append(to_columns(grad, thin_lanes))
        thin_send[3 - number] = jnp.concatenate(packed, axis=1).astype(BF16)
        send_all(6 - 2 * number, *exchanges[6 - 2 * number])

    def gate_back(number):
        for row in range(rows):
            gate = jax.nn.sigmoid(pre[number, 4, span(row)])
            pre_grad[number, 4, span(row), :] = (
                up[number, span(row)] * update[number, span(row)] * gate * (1.0 - gate)
            ).astype(BF16)

    def weight_sum(number, part):
        if part == 5:
            grad = dot(mixture[number], update_grad[number], 0, 0)
        else:
            grad = dot(activated[number], pre_grad[number, part], 0, 0)
        grad = (grad * (1.0 / residues)).astype(BF16)
        if number == 0 and part < 4:
            late_send[pl.ds(part * channels, channels), :] = grad
        else:
            slot = part if number == 1 else part + 2
            early_send[pl.ds(slot * channels, channels), :] = grad

    def send_factor_grads(number):
        phase = 6 - 2 * number
        take_all(phase, *exchanges[phase])
        for owner in range(n):
            block = thin_recv[3 - number, owner].astype(F32)
            for place, (first, last) in enumerate(halves):
                for row in range(first, last):
                    lane = (row - first) * residues
                    stage8[pl.ds((owner * rows + row) * slices, slices), :residues] = block[
                        place * slices : (place + 1) * slices, lane : lane + residues
                    ]
        for channel in range(slices):
            grad = stage8[pl.ds(channel, padded, stride=slices), :].astype(BF16)
            left, right = factors[number, 0, channel], factors[number, 1, channel]
            if number == 0:
                left_grad = dot(grad, right, 1, 0)
                right_grad = dot(grad, left, 0, 0)
            else:
                left_grad = dot(right, grad, 1, 1)
                right_grad = dot(left, grad, 1, 0)
            stage16[pl.ds(channel, padded, stride=double), :] = left_grad
            stage16[pl.ds(slices + channel, padded, stride=double), :] = right_grad
        for owner in range(n):
            wide_send[3 - number, owner] = pack(
                [
                    stage16[pl.ds((owner * rows + row) * double, double), :residues]
                    for row in range(rows)
                ],
                wide_lanes,
            ).astype(BF16)
        send_all(phase + 1, *exchanges[phase + 1])

    def take_factor_grads(number):
        phase = 7 - 2 * number
        take_all(phase, *exchanges[phase])
        rows16[...] = wide_recv[3 - number].astype(F32)
        for side in range(2):
            grad = to_rows(rows16[:, pl.ds(side * slices, slices), :], pairs)
            gate = jax.nn.sigmoid(pre[number, 2 * side + 1])
            opened = mask[...] * grad * gate
            pre_grad[number, 2 * side] = opened.astype(BF16)
            pre_grad[number, 2 * side + 1] = (
                opened * pre[number, 2 * side] * (1.0 - gate)
            ).astype(BF16)

    def stream_back(number):
        inner = dot(pre_grad[number, 0], proj_ref[number, 0], 1, 1)
        for part in range(1, 5):
            inner = inner + dot(pre_grad[number, part], proj_ref[number, part], 1, 1)
        mix_grad[...] = inner
        gain = gain_ref[number, 0:1, :]
        for row in range(rows):
            grad = up[number, span(row)] + norm_lanes_back(
                mix_grad[span(row), :],
                normed_in[number, span(row), :],
                inverse_in[number, span(row), :],
                gain,
            )
            if number == 1:
                up[0, span(row), :] = grad
            else:
                grad_out[row] = grad.astype(BF16)

    def send_total(phase, parts, share):
        take_all(phase, *exchanges[phase])
        result = parts[0].astype(F32)
        for owner in range(1, n):
            result = result + parts[owner].astype(F32)
        share[...] = result.astype(BF16)
        send_all(phase + 1, *exchanges[phase + 1])

    def take_total(phase, blocks):
        take_all(phase, *exchanges[phase])
        share = blocks.shape[1]
        for owner in range(n):
            total[pl.ds(owner * share, share), :] = blocks[owner].astype(F32)

    def part_of(slot):
        return total[pl.ds(slot * channels, channels), :]

    send_factors(0)
    up[1] = cot_ref[...].reshape(pairs, channels).astype(F32)
    send_product(0)
    take_product(0)
    take_update(0)
    for row in range(rows):
        gate = jax.nn.sigmoid(pre[0, 4, span(row)])
        stream[1, span(row), :] = (
            (stream[0, span(row), :] + gate * update[0, span(row)]).astype(BF16).astype(F32)
        )
    send_factors(1)
    mixture_back(1)
    send_product(1)
    take_product(1)
    send_product_grad(1)
    take_update(1)
    gate_back(1)
    send_factor_grads(1)
    weight_sum(1, 4)
    weight_sum(1, 5)
    take_factor_grads(1)
    stream_back(1)
    mixture_back(0)
    send_product_grad(0)
    gate_back(0)
    for part in range(4):
        weight_sum(1, part)
    weight_sum(0, 4)
    weight_sum(0, 5)
    send_all(8, *exchanges[8])
    send_factor_grads(0)
    send_total(8, early_recv, early_share)
    take_factor_grads(0)
    for part in range(4):
        weight_sum(0, part)
    send_all(10, *exchanges[10])
    stream_back(0)
    take_total(9, early_all)
    for part in range(5):
        proj_out[1, part] = part_of(part)
    weight_out[1] = part_of(5)
    proj_out[0, 4] = part_of(6)
    weight_out[0] = part_of(7)
    send_total(10, late_recv, late_share)
    take_total(11, late_all)
    for part in range(4):
        proj_out[0, part] = part_of(part)
    for phase in range(12):
        end_all(phase, *exchanges[phase])


def fused(
    pair_state,
    chain_index,
    pair_mask,
    chain_table,
    norm_gain,
    norm_shift,
    projections,
    output_weight,
    cotangent,
):
    rows, residues, channels = pair_state.shape
    n = lax.axis_size("dap")
    slices = channels // n
    padded = -(-residues // LANES) * LANES
    pairs = rows * residues
    double = 2 * slices
    wide = -(-pairs // LANES) * LANES
    thin = -(-((rows + 1) // 2) * residues // LANES) * LANES
    early, late = 8 * channels // n, 4 * channels // n
    vmem = pl.BlockSpec(memory_space=pltpu.VMEM)
    return pl.pallas_call(
        functools.partial(fused_kernel, n, rows, residues),
        out_shape=(
            jax.ShapeDtypeStruct((rows, residues, channels), BF16),
            jax.ShapeDtypeStruct((2, 5, channels, channels), F32),
            jax.ShapeDtypeStruct((2, channels, channels), F32),
        ),
        in_specs=[pl.BlockSpec(memory_space=pltpu.HBM)] * 9,
        out_specs=(vmem,) * 3,
        scratch_shapes=[
            pltpu.VMEM((2, pairs, channels), F32),
            pltpu.VMEM((pairs, channels), F32),
            pltpu.VMEM((2, pairs, channels), F32),
            pltpu.VMEM((2, pairs, channels), F32),
            pltpu.VMEM((2, pairs, channels), F32),
            pltpu.VMEM((2, pairs, channels), F32),
            pltpu.VMEM((2, pairs, channels), BF16),
            pltpu.VMEM((2, 5, pairs, channels), F32),
            pltpu.VMEM((2, pairs, channels), BF16),
            pltpu.VMEM((2, pairs, channels), F32),
            pltpu.VMEM((2, pairs, channels), F32),
            pltpu.VMEM((pairs, channels), F32),
            pltpu.VMEM((2, pairs, channels), BF16),
            pltpu.VMEM((2, 5, pairs, channels), BF16),
            pltpu.VMEM((2, 2, slices, padded, padded), BF16),
            pltpu.VMEM((padded * 2 * slices, padded), F32),
            pltpu.VMEM((padded * slices, padded), F32),
            pltpu.VMEM((n, double, wide), F32),
            pltpu.VMEM((n, double, thin), F32),
            pltpu.VMEM((4, n, double, wide), BF16),
            pltpu.VMEM((4, n, double, wide), BF16),
            pltpu.VMEM((4, n, double, thin), BF16),
            pltpu.VMEM((4, n, double, thin), BF16),
            pltpu.VMEM((8 * channels, channels), BF16),
            pltpu.VMEM((4 * channels, channels), BF16),
            pltpu.VMEM((n, early, channels), BF16),
            pltpu.VMEM((n, late, channels), BF16),
            pltpu.VMEM((early, channels), BF16),
            pltpu.VMEM((late, channels), BF16),
            pltpu.VMEM((n, early, channels), BF16),
            pltpu.VMEM((n, late, channels), BF16),
            pltpu.VMEM((8 * channels, channels), F32),
            pltpu.SemaphoreType.DMA((12, n)),
            pltpu.SemaphoreType.DMA((12, n)),
            pltpu.SemaphoreType.DMA((9,)),
            pltpu.VMEM((rows, residues, channels), BF16),
            pltpu.VMEM((1, residues), jnp.int32),
            pltpu.VMEM((rows, residues), jnp.int32),
            pltpu.VMEM((2, channels), F32),
            pltpu.VMEM((2, 2, channels), F32),
            pltpu.VMEM((2, 2, channels), F32),
            pltpu.VMEM((2, 5, channels, channels), BF16),
            pltpu.VMEM((2, channels, channels), BF16),
            pltpu.VMEM((rows, residues, channels), BF16),
        ],
        compiler_params=pltpu.CompilerParams(
            collective_id=0, has_side_effects=True, vmem_limit_bytes=63 * 2**20
        ),
    )(
        pair_state,
        chain_index.reshape(1, residues),
        pair_mask,
        chain_table,
        norm_gain,
        norm_shift,
        projections,
        output_weight,
        cotangent,
    )


def fits(rows, residues, channels, n):
    padded = -(-residues // LANES) * LANES
    return (
        channels == LANES
        and channels % n == 0
        and (channels // n) % 8 == 0
        and (4 * channels // n) % 16 == 0
        and n % 2 == 0
        and residues % 16 == 0
        and padded <= 2 * LANES
    )


def shards(*arguments):
    rows, residues, channels = arguments[0].shape
    n = lax.axis_size("dap")
    if fits(rows, residues, channels, n):
        return fused(*arguments)
    return sharded_ops(*arguments)


def solution(mesh):
    return jax.shard_map(
        shards,
        mesh=mesh,
        in_specs=(
            P(("groups", "dap"), None, None),
            P("groups"),
            P(("groups", "dap"), None),
            P(),
            P(),
            P(),
            P(),
            P(),
            P(("groups", "dap"), None, None),
        ),
        out_specs=(
            P(("groups", "dap"), None, None),
            P("groups", None, None, None),
            P("groups", None, None),
        ),
        check_vma=False,
    )
```

```python
import functools

import jax
import jax.numpy as jnp
from jax import lax
from jax.experimental import pallas as pl
from jax.experimental.pallas import tpu as pltpu
from jax.sharding import PartitionSpec as P

EPSILON = 1e-05


def normalize(values, norm_gain, norm_shift, reduce_axis):
    center = values - jnp.mean(values, axis=reduce_axis, keepdims=True)
    inverse = lax.rsqrt(jnp.mean(center * center, axis=reduce_axis, keepdims=True) + EPSILON)
    normed = center * inverse
    return (normed, inverse, normed * norm_gain + norm_shift)


def normalize_back(grad_output, normed, inverse, norm_gain, reduce_axis):
    scaled = grad_output * norm_gain
    centered = scaled - jnp.mean(scaled, axis=reduce_axis, keepdims=True)
    return (
        centered - normed * jnp.mean(scaled * normed, axis=reduce_axis, keepdims=True)
    ) * inverse


def multiply(left_cols, right_cols, incoming):
    if incoming:
        return jnp.einsum(
            "xcki,xckj->xcij", left_cols, right_cols, preferred_element_type=jnp.float32
        )
    return jnp.einsum("xcik,xcjk->xcij", left_cols, right_cols, preferred_element_type=jnp.float32)


def factor_grads(grad_cols, left_cols, right_cols, incoming):
    if incoming:
        left_grad = jnp.einsum(
            "xcij,xckj->xcki", grad_cols, right_cols, preferred_element_type=jnp.float32
        )
        right_grad = jnp.einsum(
            "xcij,xcki->xckj", grad_cols, left_cols, preferred_element_type=jnp.float32
        )
    else:
        left_grad = jnp.einsum(
            "xcij,xcjk->xcik", grad_cols, right_cols, preferred_element_type=jnp.float32
        )
        right_grad = jnp.einsum(
            "xcij,xcik->xcjk", grad_cols, left_cols, preferred_element_type=jnp.float32
        )
    return (left_grad.astype(jnp.bfloat16), right_grad.astype(jnp.bfloat16))


def block_forward(stream, masked, norm_gains, norm_shifts, weights, out_weight, incoming):
    rows, residues, channels = stream.shape
    devices = lax.axis_size("dap")
    slices = channels // devices
    normed_in, inverse_in, scaled_in = normalize(stream, norm_gains[0], norm_shifts[0], 2)
    activated = scaled_in.astype(jnp.bfloat16)
    factor_pre = jnp.einsum(
        "rnd,pdc->pcrn", activated, weights[:4], preferred_element_type=jnp.float32
    )
    gate_pre = jnp.einsum("rnd,dc->rnc", activated, weights[4], preferred_element_type=jnp.float32)
    gate_left = jax.nn.sigmoid(factor_pre[1])
    gate_right = jax.nn.sigmoid(factor_pre[3])
    left_factor = (masked * gate_left * factor_pre[0]).astype(jnp.bfloat16)
    right_factor = (masked * gate_right * factor_pre[2]).astype(jnp.bfloat16)
    left_blocks = left_factor.reshape(devices, slices, rows, residues)
    right_blocks = right_factor.reshape(devices, slices, rows, residues)
    left_cols, right_cols = (
        lax.all_to_all(left_blocks, "dap", split_axis=0, concat_axis=2, tiled=True),
        lax.all_to_all(right_blocks, "dap", split_axis=0, concat_axis=2, tiled=True),
    )
    product = multiply(left_cols, right_cols, incoming).astype(jnp.bfloat16)
    returned = lax.all_to_all(product, "dap", split_axis=2, concat_axis=0, tiled=True)
    product_rows = returned.reshape(channels, rows, residues)
    normed_out, inverse_out, scaled_out = normalize(
        product_rows.astype(jnp.float32),
        norm_gains[1][:, None, None],
        norm_shifts[1][:, None, None],
        0,
    )
    mixture = scaled_out.astype(jnp.bfloat16)
    update = jnp.einsum("crn,cd->rnd", mixture, out_weight, preferred_element_type=jnp.float32)
    out_gate = jax.nn.sigmoid(gate_pre)
    following = (stream + out_gate * update).astype(jnp.bfloat16)
    stored = (
        activated,
        factor_pre,
        left_cols,
        right_cols,
        normed_out,
        inverse_out,
        mixture,
        update,
        out_gate,
        normed_in,
        inverse_in,
    )
    return (following, stored)


def block_backward(upstream, stored, masked, norm_gains, weights, out_weight, incoming):
    (
        activated,
        factor_pre,
        left_cols,
        right_cols,
        normed_out,
        inverse_out,
        mixture,
        update,
        out_gate,
        normed_in,
        inverse_in,
    ) = stored
    rows, residues, channels = upstream.shape
    devices = lax.axis_size("dap")
    slices = channels // devices
    update_grad = (upstream * out_gate).astype(jnp.bfloat16)
    gate_grad = (upstream * update * out_gate * (1.0 - out_gate)).astype(jnp.bfloat16)
    out_weight_grad = jnp.einsum(
        "crn,rnd->cd", mixture, update_grad, preferred_element_type=jnp.float32
    )
    mixture_grad = jnp.einsum(
        "rnd,cd->crn", update_grad, out_weight, preferred_element_type=jnp.float32
    )
    product_grad = normalize_back(
        mixture_grad, normed_out, inverse_out, norm_gains[1][:, None, None], 0
    ).astype(jnp.bfloat16)
    grad_blocks = product_grad.reshape(devices, slices, rows, residues)
    grad_cols = lax.all_to_all(grad_blocks, "dap", split_axis=0, concat_axis=2, tiled=True)
    left_grad, right_grad = factor_grads(grad_cols, left_cols, right_cols, incoming)
    left_back, right_back = (
        lax.all_to_all(left_grad, "dap", split_axis=2, concat_axis=0, tiled=True),
        lax.all_to_all(right_grad, "dap", split_axis=2, concat_axis=0, tiled=True),
    )
    left_rows = left_back.reshape(channels, rows, residues).astype(jnp.float32)
    right_rows = right_back.reshape(channels, rows, residues).astype(jnp.float32)
    gate_left = jax.nn.sigmoid(factor_pre[1])
    gate_right = jax.nn.sigmoid(factor_pre[3])
    factor_grad = jnp.stack(
        [
            left_rows * masked * gate_left,
            left_rows * masked * factor_pre[0] * gate_left * (1.0 - gate_left),
            right_rows * masked * gate_right,
            right_rows * masked * factor_pre[2] * gate_right * (1.0 - gate_right),
        ]
    ).astype(jnp.bfloat16)
    factor_weight_grads = jnp.einsum(
        "rnd,pcrn->pdc", activated, factor_grad, preferred_element_type=jnp.float32
    )
    gate_weight_grad = jnp.einsum(
        "rnd,rnc->dc", activated, gate_grad, preferred_element_type=jnp.float32
    )
    weight_grads = jnp.concatenate([factor_weight_grads, gate_weight_grad[None]], 0)
    input_grad = jnp.einsum(
        "pcrn,pdc->rnd", factor_grad, weights[:4], preferred_element_type=jnp.float32
    )
    input_grad = input_grad + jnp.einsum(
        "rnc,dc->rnd", gate_grad, weights[4], preferred_element_type=jnp.float32
    )
    stream_grad = upstream + normalize_back(input_grad, normed_in, inverse_in, norm_gains[0], 2)
    return (stream_grad, weight_grads, out_weight_grad)


def reduce_block(weight_grads, out_weight_grad):
    return lax.psum((weight_grads, out_weight_grad), "dap")


def sharded_ops(
    pair_state,
    chain_index,
    pair_mask,
    chain_table,
    norm_gain,
    norm_shift,
    projections,
    output_weight,
    cotangent,
):
    rows, residues, channels = pair_state.shape
    first_row = lax.axis_index("dap") * rows
    own_chain = lax.dynamic_slice_in_dim(chain_index, first_row, rows, 0)
    same_chain = own_chain[:, None] == chain_index[None, :]
    stream = pair_state.astype(jnp.float32) + jnp.where(
        same_chain[:, :, None], chain_table[1], chain_table[0]
    )
    masked = pair_mask.astype(jnp.float32)[None]
    following, stored_first = block_forward(
        stream, masked, norm_gain[0], norm_shift[0], projections[0], output_weight[0], False
    )
    ignored, stored_second = block_forward(
        following.astype(jnp.float32),
        masked,
        norm_gain[1],
        norm_shift[1],
        projections[1],
        output_weight[1],
        True,
    )
    grad_mid, proj_second, out_second = block_backward(
        cotangent.astype(jnp.float32),
        stored_second,
        masked,
        norm_gain[1],
        projections[1],
        output_weight[1],
        True,
    )
    proj_second, out_second = reduce_block(proj_second, out_second)
    grad_first, proj_first, out_first = block_backward(
        grad_mid, stored_first, masked, norm_gain[0], projections[0], output_weight[0], False
    )
    proj_first, out_first = reduce_block(proj_first, out_first)
    scale_rows = 1.0 / residues
    projection_grads = jnp.stack([proj_first, proj_second]) * scale_rows
    weight_grad_out = jnp.stack([out_first, out_second]) * scale_rows
    return (grad_first.astype(jnp.bfloat16), projection_grads, weight_grad_out)


LANES = 128
F32 = jnp.float32
BF16 = jnp.bfloat16


def dot(left, right, left_dim, right_dim):
    return lax.dot_general(
        left, right, (((left_dim,), (right_dim,)), ((), ())), preferred_element_type=F32
    )


def norm_lanes(values):
    center = values - jnp.mean(values, axis=1, keepdims=True)
    inverse = lax.rsqrt(jnp.mean(center * center, axis=1, keepdims=True) + EPSILON)
    return center * inverse, inverse


def norm_lanes_back(grad, normed, inverse, gain):
    scaled = grad * gain
    centered = scaled - jnp.mean(scaled, axis=1, keepdims=True)
    return (centered - normed * jnp.mean(scaled * normed, axis=1, keepdims=True)) * inverse


def fused_kernel(
    n,
    rows,
    residues,
    pair_hbm,
    chain_hbm,
    mask_hbm,
    table_hbm,
    gain_hbm,
    shift_hbm,
    proj_hbm,
    weight_hbm,
    cot_hbm,
    grad_out,
    proj_out,
    weight_out,
    stream,
    mask,
    normed_in,
    inverse_in,
    normed_out,
    inverse_out,
    activated,
    pre,
    mixture,
    update,
    up,
    mix_grad,
    update_grad,
    pre_grad,
    factors,
    stage16,
    stage8,
    rows16,
    rows8,
    wide_send,
    wide_recv,
    thin_send,
    thin_recv,
    early_send,
    late_send,
    early_recv,
    late_recv,
    early_share,
    late_share,
    early_all,
    late_all,
    total,
    send_sem,
    recv_sem,
    load_sem,
    pair_ref,
    chain_ref,
    mask_ref,
    table_ref,
    gain_ref,
    shift_ref,
    proj_ref,
    weight_ref,
    cot_ref,
):
    channels = LANES
    slices = channels // n
    padded = factors.shape[-1]
    pairs = rows * residues
    double = 2 * slices
    me = lax.axis_index("dap")
    barrier = pltpu.get_barrier_semaphore()

    def each_peer(body, unrolled=False):
        def step(index, carry):
            body(lax.rem(me + index, n))
            return carry

        lax.fori_loop(1, n, step, 0, unroll=n - 1 if unrolled else 1)

    def greet(peer):
        pl.semaphore_signal(
            barrier, inc=1, device_id={"dap": peer}, device_id_type=pl.DeviceIdType.MESH
        )

    each_peer(greet)
    loads = [
        pltpu.make_async_copy(source, target, load_sem.at[place])
        for place, (source, target) in enumerate(
            (
                (chain_hbm, chain_ref),
                (mask_hbm, mask_ref),
                (table_hbm, table_ref),
                (pair_hbm, pair_ref),
                (gain_hbm, gain_ref),
                (shift_hbm, shift_ref),
                (proj_hbm, proj_ref),
                (weight_hbm, weight_ref),
                (cot_hbm, cot_ref),
            )
        )
    ]
    for load in loads:
        load.start()

    def copy(phase, source, target, peer, owner):
        return pltpu.make_async_remote_copy(
            src_ref=source,
            dst_ref=target.at[owner],
            send_sem=send_sem.at[phase, peer],
            recv_sem=recv_sem.at[phase, owner],
            device_id={"dap": peer},
            device_id_type=pl.DeviceIdType.MESH,
        )

    def send_all(phase, source_of, target):
        each_peer(lambda peer: copy(phase, source_of(peer), target, peer, me).start(), True)
        target[me] = source_of(me)[...]

    def take_all(phase, source_of, target):
        each_peer(lambda peer: copy(phase, source_of(peer), target, peer, peer).wait_recv())

    def end_all(phase, source_of, target):
        each_peer(lambda peer: copy(phase, source_of(peer), target, peer, me).wait_send())

    def span(row):
        return pl.ds(row * residues, residues)

    upper = (rows + 1) // 2
    halves = ((0, upper), (upper, rows))
    wide_lanes = wide_send.shape[-1]
    thin_lanes = thin_send.shape[-1]

    def to_columns(values, lanes):
        filler = jnp.zeros((lanes - values.shape[0], channels), F32)
        return jnp.concatenate([values, filler], axis=0).T.reshape(n, slices, lanes)

    def to_rows(blocks, count):
        return blocks.reshape(channels, blocks.shape[-1]).T[:count]

    def pack(tiles, lanes):
        filler = jnp.zeros((tiles[0].shape[0], lanes - len(tiles) * residues), F32)
        return jnp.concatenate(tiles + [filler], axis=1)

    def wide(number):
        return lambda peer: wide_send.at[number, peer]

    def thin(number):
        return lambda peer: thin_send.at[number, peer]

    def shares(sums, share):
        return lambda peer: sums.at[pl.ds(pl.multiple_of(peer * share, 16), share)]

    exchanges = {
        0: (wide(0), wide_recv.at[0]),
        1: (thin(0), thin_recv.at[0]),
        2: (wide(1), wide_recv.at[1]),
        3: (thin(1), thin_recv.at[1]),
        4: (thin(2), thin_recv.at[2]),
        5: (wide(2), wide_recv.at[2]),
        6: (thin(3), thin_recv.at[3]),
        7: (wide(3), wide_recv.at[3]),
        8: (shares(early_send, early_recv.shape[1]), early_recv),
        9: (lambda peer: early_share, early_all),
        10: (shares(late_send, late_recv.shape[1]), late_recv),
        11: (lambda peer: late_share, late_all),
    }

    stage16[...] = jnp.zeros_like(stage16)
    stage8[...] = jnp.zeros_like(stage8)

    for load in loads:
        load.wait()
    chain = chain_ref[...]
    place = lax.broadcasted_iota(jnp.int32, chain.shape, 1)
    for row in range(rows):
        own = jnp.sum(jnp.where(place == me * rows + row, chain, 0), axis=1, keepdims=True)
        same = jnp.where(chain == own, 1.0, 0.0).astype(F32)
        filler = jnp.zeros((1, padded - residues), F32)
        seen = mask_ref[pl.ds(row, 1), :].astype(F32)
        if padded > residues:
            same = jnp.concatenate([same, filler], axis=1)
            seen = jnp.concatenate([seen, filler], axis=1)
        same = jnp.broadcast_to(same, (channels, padded)).T[:residues]
        mask[span(row), :] = jnp.broadcast_to(seen, (channels, padded)).T[:residues]
        stream[0, span(row), :] = pair_ref[row].astype(F32) + jnp.where(
            same > 0.5, table_ref[1:2, :], table_ref[0:1, :]
        )

    def send_factors(number):
        gain, shift = gain_ref[number, 0:1, :], shift_ref[number, 0:1, :]
        for row in range(rows):
            normed, inverse = norm_lanes(stream[number, span(row), :])
            normed_in[number, span(row), :] = normed
            inverse_in[number, span(row), :] = jnp.broadcast_to(inverse, normed.shape)
            activated[number, span(row), :] = (normed * gain + shift).astype(BF16)
        for part in range(5):
            pre[number, part] = dot(activated[number], proj_ref[number, part], 1, 0)
        left = mask[...] * jax.nn.sigmoid(pre[number, 1]) * pre[number, 0]
        right = mask[...] * jax.nn.sigmoid(pre[number, 3]) * pre[number, 2]
        both = jnp.concatenate(
            [to_columns(left, wide_lanes), to_columns(right, wide_lanes)], axis=1
        )
        wide_send[number] = both.astype(BF16)
        if number == 0:
            pl.semaphore_wait(barrier, n - 1)
        send_all(2 * number, *exchanges[2 * number])

    def send_product(number):
        take_all(2 * number, *exchanges[2 * number])
        for owner in range(n):
            block = wide_recv[number, owner].astype(F32)
            for row in range(rows):
                stage16[pl.ds((owner * rows + row) * double, double), :residues] = block[
                    :, row * residues : (row + 1) * residues
                ]
        for channel in range(slices):
            left = stage16[pl.ds(channel, padded, stride=double), :].astype(BF16)
            right = stage16[pl.ds(slices + channel, padded, stride=double), :].astype(BF16)
            factors[number, 0, channel] = left
            factors[number, 1, channel] = right
            stage8[pl.ds(channel, padded, stride=slices), :] = dot(
                left, right, 1 - number, 1 - number
            )
        for owner in range(n):
            packed = [
                pack(
                    [
                        stage8[pl.ds((owner * rows + row) * slices, slices), :residues]
                        for row in range(*half)
                    ],
                    thin_lanes,
                )
                for half in halves
            ]
            thin_send[number, owner] = jnp.concatenate(packed, axis=0).astype(BF16)
        send_all(2 * number + 1, *exchanges[2 * number + 1])

    def take_product(number):
        take_all(2 * number + 1, *exchanges[2 * number + 1])
        gain, shift = gain_ref[number, 1:2, :], shift_ref[number, 1:2, :]
        rows8[...] = thin_recv[number].astype(F32)
        for place, (first, last) in enumerate(halves):
            count = (last - first) * residues
            product = to_rows(rows8[:, pl.ds(place * slices, slices), :], count)
            normed, inverse = norm_lanes(product)
            where = pl.ds(first * residues, count)
            normed_out[number, where, :] = normed
            inverse_out[number, where, :] = jnp.broadcast_to(inverse, normed.shape)
            mixture[number, where, :] = (normed * gain + shift).astype(BF16)

    def take_update(number):
        update[number] = dot(mixture[number], weight_ref[number], 1, 0)

    def mixture_back(number):
        for row in range(rows):
            gate = jax.nn.sigmoid(pre[number, 4, span(row)])
            update_grad[number, span(row), :] = (up[number, span(row)] * gate).astype(BF16)
        mix_grad[...] = dot(update_grad[number], weight_ref[number], 1, 1)

    def send_product_grad(number):
        gain = gain_ref[number, 1:2, :]
        packed = []
        for first, last in halves:
            where = pl.ds(first * residues, (last - first) * residues)
            grad = norm_lanes_back(
                mix_grad[where, :],
                normed_out[number, where, :],
                inverse_out[number, where, :],
                gain,
            )
            packed.append(to_columns(grad, thin_lanes))
        thin_send[3 - number] = jnp.concatenate(packed, axis=1).astype(BF16)
        send_all(6 - 2 * number, *exchanges[6 - 2 * number])

    def gate_back(number):
        for row in range(rows):
            gate = jax.nn.sigmoid(pre[number, 4, span(row)])
            pre_grad[number, 4, span(row), :] = (
                up[number, span(row)] * update[number, span(row)] * gate * (1.0 - gate)
            ).astype(BF16)

    def weight_sum(number, part):
        if part == 5:
            grad = dot(mixture[number], update_grad[number], 0, 0)
        else:
            grad = dot(activated[number], pre_grad[number, part], 0, 0)
        grad = (grad * (1.0 / residues)).astype(BF16)
        if number == 0 and part < 4:
            late_send[pl.ds(part * channels, channels), :] = grad
        else:
            slot = part if number == 1 else part + 2
            early_send[pl.ds(slot * channels, channels), :] = grad

    def send_factor_grads(number):
        phase = 6 - 2 * number
        take_all(phase, *exchanges[phase])
        for owner in range(n):
            block = thin_recv[3 - number, owner].astype(F32)
            for place, (first, last) in enumerate(halves):
                for row in range(first, last):
                    lane = (row - first) * residues
                    stage8[pl.ds((owner * rows + row) * slices, slices), :residues] = block[
                        place * slices : (place + 1) * slices, lane : lane + residues
                    ]
        for channel in range(slices):
            grad = stage8[pl.ds(channel, padded, stride=slices), :].astype(BF16)
            left, right = factors[number, 0, channel], factors[number, 1, channel]
            if number == 0:
                left_grad = dot(grad, right, 1, 0)
                right_grad = dot(grad, left, 0, 0)
            else:
                left_grad = dot(right, grad, 1, 1)
                right_grad = dot(left, grad, 1, 0)
            stage16[pl.ds(channel, padded, stride=double), :] = left_grad
            stage16[pl.ds(slices + channel, padded, stride=double), :] = right_grad
        for owner in range(n):
            wide_send[3 - number, owner] = pack(
                [
                    stage16[pl.ds((owner * rows + row) * double, double), :residues]
                    for row in range(rows)
                ],
                wide_lanes,
            ).astype(BF16)
        send_all(phase + 1, *exchanges[phase + 1])

    def take_factor_grads(number):
        phase = 7 - 2 * number
        take_all(phase, *exchanges[phase])
        rows16[...] = wide_recv[3 - number].astype(F32)
        for side in range(2):
            grad = to_rows(rows16[:, pl.ds(side * slices, slices), :], pairs)
            gate = jax.nn.sigmoid(pre[number, 2 * side + 1])
            opened = mask[...] * grad * gate
            pre_grad[number, 2 * side] = opened.astype(BF16)
            pre_grad[number, 2 * side + 1] = (
                opened * pre[number, 2 * side] * (1.0 - gate)
            ).astype(BF16)

    def stream_back(number):
        inner = dot(pre_grad[number, 0], proj_ref[number, 0], 1, 1)
        for part in range(1, 5):
            inner = inner + dot(pre_grad[number, part], proj_ref[number, part], 1, 1)
        mix_grad[...] = inner
        gain = gain_ref[number, 0:1, :]
        for row in range(rows):
            grad = up[number, span(row)] + norm_lanes_back(
                mix_grad[span(row), :],
                normed_in[number, span(row), :],
                inverse_in[number, span(row), :],
                gain,
            )
            if number == 1:
                up[0, span(row), :] = grad
            else:
                grad_out[row] = grad

    def send_total(phase, parts, share):
        take_all(phase, *exchanges[phase])
        result = parts[0].astype(F32)
        for owner in range(1, n):
            result = result + parts[owner].astype(F32)
        share[...] = result.astype(BF16)
        send_all(phase + 1, *exchanges[phase + 1])

    def take_total(phase, blocks):
        take_all(phase, *exchanges[phase])
        share = blocks.shape[1]
        for owner in range(n):
            total[pl.ds(owner * share, share), :] = blocks[owner]

    def part_of(slot):
        return total[pl.ds(slot * channels, channels), :]

    send_factors(0)
    up[1] = cot_ref[...].reshape(pairs, channels).astype(F32)
    send_product(0)
    take_product(0)
    take_update(0)
    for row in range(rows):
        gate = jax.nn.sigmoid(pre[0, 4, span(row)])
        stream[1, span(row), :] = (
            (stream[0, span(row), :] + gate * update[0, span(row)]).astype(BF16).astype(F32)
        )
    send_factors(1)
    mixture_back(1)
    send_product(1)
    take_product(1)
    send_product_grad(1)
    take_update(1)
    gate_back(1)
    send_factor_grads(1)
    weight_sum(1, 4)
    weight_sum(1, 5)
    take_factor_grads(1)
    stream_back(1)
    mixture_back(0)
    send_product_grad(0)
    gate_back(0)
    for part in range(4):
        weight_sum(1, part)
    weight_sum(0, 4)
    weight_sum(0, 5)
    send_all(8, *exchanges[8])
    send_factor_grads(0)
    send_total(8, early_recv, early_share)
    take_factor_grads(0)
    for part in range(4):
        weight_sum(0, part)
    send_all(10, *exchanges[10])
    stream_back(0)
    take_total(9, early_all)
    for part in range(5):
        proj_out[1, part] = part_of(part)
    weight_out[1] = part_of(5)
    proj_out[0, 4] = part_of(6)
    weight_out[0] = part_of(7)
    send_total(10, late_recv, late_share)
    take_total(11, late_all)
    for part in range(4):
        proj_out[0, part] = part_of(part)
    for phase in range(12):
        end_all(phase, *exchanges[phase])


def fused(
    pair_state,
    chain_index,
    pair_mask,
    chain_table,
    norm_gain,
    norm_shift,
    projections,
    output_weight,
    cotangent,
):
    rows, residues, channels = pair_state.shape
    n = lax.axis_size("dap")
    slices = channels // n
    padded = -(-residues // LANES) * LANES
    pairs = rows * residues
    double = 2 * slices
    wide = -(-pairs // LANES) * LANES
    thin = -(-((rows + 1) // 2) * residues // LANES) * LANES
    early, late = 8 * channels // n, 4 * channels // n
    vmem = pl.BlockSpec(memory_space=pltpu.VMEM)
    grad, proj, weight = pl.pallas_call(
        functools.partial(fused_kernel, n, rows, residues),
        out_shape=(
            jax.ShapeDtypeStruct((rows, residues, channels), F32),
            jax.ShapeDtypeStruct((2, 5, channels, channels), BF16),
            jax.ShapeDtypeStruct((2, channels, channels), BF16),
        ),
        in_specs=[pl.BlockSpec(memory_space=pltpu.HBM)] * 9,
        out_specs=(vmem,) * 3,
        scratch_shapes=[
            pltpu.VMEM((2, pairs, channels), F32),
            pltpu.VMEM((pairs, channels), F32),
            pltpu.VMEM((2, pairs, channels), F32),
            pltpu.VMEM((2, pairs, channels), F32),
            pltpu.VMEM((2, pairs, channels), F32),
            pltpu.VMEM((2, pairs, channels), F32),
            pltpu.VMEM((2, pairs, channels), BF16),
            pltpu.VMEM((2, 5, pairs, channels), F32),
            pltpu.VMEM((2, pairs, channels), BF16),
            pltpu.VMEM((2, pairs, channels), F32),
            pltpu.VMEM((2, pairs, channels), F32),
            pltpu.VMEM((pairs, channels), F32),
            pltpu.VMEM((2, pairs, channels), BF16),
            pltpu.VMEM((2, 5, pairs, channels), BF16),
            pltpu.VMEM((2, 2, slices, padded, padded), BF16),
            pltpu.VMEM((padded * 2 * slices, padded), F32),
            pltpu.VMEM((padded * slices, padded), F32),
            pltpu.VMEM((n, double, wide), F32),
            pltpu.VMEM((n, double, thin), F32),
            pltpu.VMEM((4, n, double, wide), BF16),
            pltpu.VMEM((4, n, double, wide), BF16),
            pltpu.VMEM((4, n, double, thin), BF16),
            pltpu.VMEM((4, n, double, thin), BF16),
            pltpu.VMEM((8 * channels, channels), BF16),
            pltpu.VMEM((4 * channels, channels), BF16),
            pltpu.VMEM((n, early, channels), BF16),
            pltpu.VMEM((n, late, channels), BF16),
            pltpu.VMEM((early, channels), BF16),
            pltpu.VMEM((late, channels), BF16),
            pltpu.VMEM((n, early, channels), BF16),
            pltpu.VMEM((n, late, channels), BF16),
            pltpu.VMEM((8 * channels, channels), BF16),
            pltpu.SemaphoreType.DMA((12, n)),
            pltpu.SemaphoreType.DMA((12, n)),
            pltpu.SemaphoreType.DMA((9,)),
            pltpu.VMEM((rows, residues, channels), BF16),
            pltpu.VMEM((1, residues), jnp.int32),
            pltpu.VMEM((rows, residues), jnp.int32),
            pltpu.VMEM((2, channels), F32),
            pltpu.VMEM((2, 2, channels), F32),
            pltpu.VMEM((2, 2, channels), F32),
            pltpu.VMEM((2, 5, channels, channels), BF16),
            pltpu.VMEM((2, channels, channels), BF16),
            pltpu.VMEM((rows, residues, channels), BF16),
        ],
        compiler_params=pltpu.CompilerParams(
            collective_id=0, has_side_effects=True, vmem_limit_bytes=63 * 2**20
        ),
    )(
        pair_state,
        chain_index.reshape(1, residues),
        pair_mask,
        chain_table,
        norm_gain,
        norm_shift,
        projections,
        output_weight,
        cotangent,
    )
    return grad.astype(BF16), proj.astype(F32), weight.astype(F32)


def fits(rows, residues, channels, n):
    padded = -(-residues // LANES) * LANES
    return (
        channels == LANES
        and channels % n == 0
        and (channels // n) % 8 == 0
        and (4 * channels // n) % 16 == 0
        and n % 2 == 0
        and residues % 16 == 0
        and padded <= 2 * LANES
    )


def shards(*arguments):
    rows, residues, channels = arguments[0].shape
    n = lax.axis_size("dap")
    if fits(rows, residues, channels, n):
        return fused(*arguments)
    return sharded_ops(*arguments)


def solution(mesh):
    return jax.shard_map(
        shards,
        mesh=mesh,
        in_specs=(
            P(("groups", "dap"), None, None),
            P("groups"),
            P(("groups", "dap"), None),
            P(),
            P(),
            P(),
            P(),
            P(),
            P(("groups", "dap"), None, None),
        ),
        out_specs=(
            P(("groups", "dap"), None, None),
            P("groups", None, None, None),
            P("groups", None, None),
        ),
        check_vma=False,
    )
```
